32 devices in a mesh: ty: 4 (over z), tx: 8 (over y, x, core).
Axes of the slice: x: 2, y: 2, z: 4, core: 2. Of those that a mesh axis runs over, the one named last changes fastest.
Arguments:
- strips: bfloat16 [2, 4, 8, 4, 8, 128, 128], P(None, 'ty', 'tx'), may hold values from -6 to 6
- centers: bfloat16 [2, 4, 8, 8, 128, 128], P(None, 'ty', 'tx'), may hold values from -6 to 6
- match_lists: int32 [2, 4, 8, 5, 8, 2], P(None, 'ty', 'tx'), may hold values from 0 to 1023, as said below
- match_counts: int32 [2, 4, 8, 5], P(None, 'ty', 'tx'), may hold values from 0 to 8, as said below
- spring_stiffness: float32 [2, 4, 8], P(None, 'ty', 'tx'), may hold values from 0.5 to 6
Outputs:
- vertex_shift: float32 [2, 2, 4, 8, 1024], P(None, None, 'ty', 'tx')
- match_shift: float32 [2, 2, 4, 8, 5, 8], P(None, None, 'ty', 'tx')
The draws below stay inside these ranges and needn't reach their ends.
Inputs may be any that keep to these rules, and one draw needn't show every extreme that they name: `match_lists`: entry [s, r, c, k, j, 0] is a vertex of tile (r, c) of section s and entry [s, r, c, k, j, 1] a vertex of its partner tile in direction k. The lists are mirrored: slot j of the east list of tile (r, c) equals slot j of the west list of tile (r, c+1) with its two vertices swapped; likewise south and north lists, and the cross lists of the two sections. `match_counts`: slots j below the count are matches, the others are unused. Counts are mirrored like the lists, and are 0 in directions that leave the slab.
All inputs are finite; a program needn't handle non-finite values.
Results may differ from the reference program's by a relative error of at most 0.0003.
Values may be sent and summed in bfloat16 or wider, within the bound.
A program may use at most 128 MiB of HBM per device.

```python
import jax
import jax.numpy as jnp
from jax import lax

P_SIZE = 8
W = 128
V = 32
ITERS = 3
NTR = 4
NTC = 8


binomial_weights = (1.0, 6.0, 15.0, 20.0, 15.0, 6.0, 1.0)


unit_rescale = 4096.0 / 924.0


def smooth_field(field):
    for along in (-2, -1):
        total = jnp.zeros_like(field)
        for offset, factor in enumerate(binomial_weights):
            total = total + factor / 64.0 * jnp.roll(field, offset - 3, axis=along)
        field = total
    return field * unit_rescale


def texture(subkey, dims):
    base = jax.random.normal(subkey, dims, jnp.float32)
    return smooth_field(base)


def speckle(subkey, dims):
    return jax.random.normal(subkey, dims, jnp.float32)


def roll_patches(patches, offsets):

    def roll_single(patch, offset):
        return jnp.roll(jnp.roll(patch, offset[0], axis=0), offset[1], axis=1)
    flat = patches.reshape((-1, W, W))
    moved = jax.vmap(roll_single)(flat, offsets.reshape((-1, 2)))
    return moved.reshape(patches.shape)


def subpixel(patches, fractions):
    row_part = fractions[..., 0][..., None, None]
    col_part = fractions[..., 1][..., None, None]
    moved = (1.0 - row_part) * patches + row_part * jnp.roll(patches, 1, axis=-2)
    return (1.0 - col_part) * moved + col_part * jnp.roll(moved, 1, axis=-1)


def pixel_fields(key):
    subkeys = [jax.random.fold_in(key, 501 + number) for number in range(17)]
    edge_dims = (2, NTR, NTC, P_SIZE, W, W)
    largest_lag = W // 4
    east_tissue = texture(subkeys[0], edge_dims)
    south_tissue = texture(subkeys[1], edge_dims)
    cross_tissue = texture(subkeys[2], (NTR, NTC, P_SIZE, W, W))
    lags_east = jax.random.randint(subkeys[3], (2, NTR, NTC, P_SIZE, 2), -largest_lag, largest_lag + 1)
    lags_south = jax.random.randint(subkeys[4], (2, NTR, NTC, P_SIZE, 2), -largest_lag, largest_lag + 1)
    lags_cross = jax.random.randint(subkeys[5], (NTR, NTC, P_SIZE, 2), -largest_lag, largest_lag + 1)
    parts_east = jax.random.uniform(subkeys[14], (2, NTR, NTC, P_SIZE, 2), jnp.float32, 0.0, 1.0)
    parts_south = jax.random.uniform(subkeys[15], (2, NTR, NTC, P_SIZE, 2), jnp.float32, 0.0, 1.0)
    parts_cross = jax.random.uniform(subkeys[16], (NTR, NTC, P_SIZE, 2), jnp.float32, 0.0, 1.0)
    east_side = east_tissue + speckle(subkeys[6], edge_dims)
    west_moved = subpixel(roll_patches(east_tissue, lags_east), parts_east) + speckle(subkeys[7], edge_dims)
    west_side = jnp.concatenate([texture(subkeys[8], (2, NTR, 1, P_SIZE, W, W)), west_moved[:, :, :-1]], axis=2)
    south_side = south_tissue + speckle(subkeys[9], edge_dims)
    north_moved = subpixel(roll_patches(south_tissue, lags_south), parts_south) + speckle(subkeys[10], edge_dims)
    north_side = jnp.concatenate([texture(subkeys[11], (2, 1, NTC, P_SIZE, W, W)), north_moved[:, :-1]], axis=1)
    strips = jnp.stack([east_side, west_side, south_side, north_side], axis=3)
    first_center = cross_tissue + speckle(subkeys[12], (NTR, NTC, P_SIZE, W, W))
    second_center = subpixel(roll_patches(cross_tissue, lags_cross), parts_cross) + speckle(subkeys[13], (NTR, NTC, P_SIZE, W, W))
    centers = jnp.stack([first_center, second_center])
    return (jnp.clip(strips, -6.0, 6.0), jnp.clip(centers, -6.0, 6.0))


def draw_strips(key, part):
    return pixel_fields(key)[0].astype(jnp.bfloat16)


def draw_centers(key, part):
    return pixel_fields(key)[1].astype(jnp.bfloat16)


def match_graph(key):
    subkeys = [jax.random.fold_in(key, 901 + number) for number in range(14)]
    vertices = V * V
    edge_dims = (2, NTR, NTC, P_SIZE)
    own_east = jax.random.randint(subkeys[0], edge_dims, 0, vertices)
    far_east = jax.random.randint(subkeys[1], edge_dims, 0, vertices)
    own_south = jax.random.randint(subkeys[2], edge_dims, 0, vertices)
    far_south = jax.random.randint(subkeys[3], edge_dims, 0, vertices)
    own_cross = jax.random.randint(subkeys[4], (NTR, NTC, P_SIZE), 0, vertices)
    far_cross = jax.random.randint(subkeys[5], (NTR, NTC, P_SIZE), 0, vertices)
    spares = jax.random.randint(subkeys[6], (4, 2, NTR, NTC, P_SIZE), 0, vertices)
    west_own = jnp.concatenate([spares[0][:, :, :1], far_east[:, :, :-1]], axis=2)
    west_far = jnp.concatenate([spares[1][:, :, :1], own_east[:, :, :-1]], axis=2)
    north_own = jnp.concatenate([spares[2][:, :1], far_south[:, :-1]], axis=1)
    north_far = jnp.concatenate([spares[3][:, :1], own_south[:, :-1]], axis=1)
    cross_own = jnp.stack([own_cross, far_cross])
    cross_far = jnp.stack([far_cross, own_cross])
    owners = jnp.stack([own_east, west_own, own_south, north_own, cross_own], axis=3)
    partners = jnp.stack([far_east, west_far, far_south, north_far, cross_far], axis=3)
    lists = jnp.stack([owners, partners], axis=-1)
    columns = jnp.arange(NTC, dtype=jnp.int32)
    rows_index = jnp.arange(NTR, dtype=jnp.int32)
    count_east = jax.random.randint(subkeys[7], (2, NTR, NTC), 0, P_SIZE + 1)
    count_east = jnp.where(columns[None, None, :] == NTC - 1, 0, count_east)
    count_east = count_east.at[0, 0, 0].set(P_SIZE)
    count_west = jnp.concatenate([jnp.zeros((2, NTR, 1), jnp.int32), count_east[:, :, :-1]], axis=2)
    count_south = jax.random.randint(subkeys[8], (2, NTR, NTC), 0, P_SIZE + 1)
    count_south = jnp.where(rows_index[None, :, None] == NTR - 1, 0, count_south)
    count_north = jnp.concatenate([jnp.zeros((2, 1, NTC), jnp.int32), count_south[:, :-1]], axis=1)
    count_cross = jax.random.randint(subkeys[9], (NTR, NTC), 0, P_SIZE + 1)
    count_cross = jnp.stack([count_cross, count_cross])
    counts = jnp.stack([count_east, count_west, count_south, count_north, count_cross], axis=3)
    return (lists.astype(jnp.int32), counts.astype(jnp.int32))


def draw_match_lists(key, part):
    return match_graph(key)[0]


def draw_match_counts(key, part):
    return match_graph(key)[1]


def draw_spring_stiffness(key, part):
    tile_dims = (2, NTR, NTC)
    col_ramp = (jnp.arange(NTC, dtype=jnp.float32) / NTC)[None, None, :]
    subkey = jax.random.fold_in(key, 1301)
    base = jnp.exp(jax.random.uniform(subkey, tile_dims, jnp.float32, jnp.log(0.5), jnp.log(2.0)))
    result = base * jnp.power(2.8, col_ramp)
    return result.astype(jnp.float32)


def setup_inputs(seed: int = 0) -> dict:
    key_of = jax.random.split(jax.random.key(seed), 6)
    return {
        "strips": draw_strips(jax.random.fold_in(key_of[5], 71), 0),
        "centers": draw_centers(jax.random.fold_in(key_of[5], 71), 0),
        "match_lists": draw_match_lists(jax.random.fold_in(key_of[5], 71), 0),
        "match_counts": draw_match_counts(jax.random.fold_in(key_of[5], 71), 0),
        "spring_stiffness": draw_spring_stiffness(jax.random.fold_in(key_of[5], 71), 0),
    }


precise = lax.Precision.HIGHEST
anchor_weight = 0.05
epsilon = 1e-6


def lag_values():
    indices = jnp.arange(W, dtype=jnp.int32)
    midpoint = W // 2
    lagged = jnp.where(indices < midpoint, indices, jnp.where(indices == midpoint, 0, indices - W))
    return lagged.astype(jnp.float32)


def displacement(own_pixels, partner_pixels):
    own_spec = jnp.fft.fft2(own_pixels.astype(jnp.float32))
    partner_spec = jnp.fft.fft2(partner_pixels.astype(jnp.float32))
    surface = jnp.real(jnp.fft.ifft2(own_spec * jnp.conj(partner_spec))) / W
    squared = surface * surface
    weight = squared * squared
    totals = jnp.sum(weight, axis=(-2, -1)) + epsilon
    lagged = lag_values()
    toward_rows = jnp.sum(weight * lagged[:, None], axis=(-2, -1))
    toward_cols = jnp.sum(weight * lagged[None, :], axis=(-2, -1))
    return jnp.stack([toward_rows / totals, toward_cols / totals]) * (2.0 / W)


def neighbour_sum(vector):
    column = jnp.arange(V * V, dtype=jnp.int32) % V
    single = jnp.zeros(vector.shape[:-1] + (1,), vector.dtype)
    row_zeros = jnp.zeros(vector.shape[:-1] + (V,), vector.dtype)
    from_left = jnp.concatenate([single, vector[..., :-1]], axis=-1) * (column > 0).astype(vector.dtype)
    from_right = jnp.concatenate([vector[..., 1:], single], axis=-1) * (column < V - 1).astype(vector.dtype)
    from_above = jnp.concatenate([row_zeros, vector[..., :-V]], axis=-1)
    from_below = jnp.concatenate([vector[..., V:], row_zeros], axis=-1)
    return from_left + from_right + from_above + from_below


def reference(strips, centers, match_lists, match_counts, spring_stiffness):
    north_next = jnp.concatenate([strips[:, 1:, :, 3], jnp.zeros_like(strips[:, :1, :, 3])], axis=1)

    def row_shifts(row_index):
        tile_row = lax.dynamic_index_in_dim(strips, row_index, 1, keepdims=False)
        next_row = lax.dynamic_index_in_dim(north_next, row_index, 1, keepdims=False)
        middle = lax.dynamic_index_in_dim(centers, row_index, 1, keepdims=False)
        west_next = jnp.concatenate([tile_row[:, 1:, 1], jnp.zeros_like(tile_row[:, :1, 1])], axis=1)
        east_offset = displacement(tile_row[:, :, 0], west_next)
        south_offset = displacement(tile_row[:, :, 2], next_row)
        cross_offset = displacement(middle[0], middle[1])
        return east_offset, south_offset, cross_offset

    east_rows, south_rows, cross_rows = lax.map(row_shifts, jnp.arange(NTR, dtype=jnp.int32))
    shift_east = jnp.moveaxis(east_rows, 0, 2)
    shift_south = jnp.moveaxis(south_rows, 0, 2)
    cross = jnp.moveaxis(cross_rows, 0, 1)
    shift_west = jnp.concatenate([jnp.zeros_like(shift_east[:, :, :, :1]), -shift_east[:, :, :, :-1]], axis=3)
    shift_north = jnp.concatenate([jnp.zeros_like(shift_south[:, :, :1]), -shift_south[:, :, :-1]], axis=2)
    shift_cross = jnp.stack([cross, -cross], axis=1)
    match_shift = jnp.stack([shift_east, shift_west, shift_south, shift_north, shift_cross], axis=4)

    valid = (jnp.arange(P_SIZE, dtype=jnp.int32) < match_counts[..., None]).astype(jnp.float32)
    vertex_ids = jnp.arange(V * V, dtype=jnp.int32)
    own_table = (match_lists[..., 0, None] == vertex_ids).astype(jnp.float32) * valid[..., None]
    partner_table = (match_lists[..., 1, None] == vertex_ids).astype(jnp.float32)
    stiffness = spring_stiffness[..., None]
    degree = neighbour_sum(jnp.ones((V * V,), jnp.float32))
    diagonal = anchor_weight + stiffness * degree + jnp.sum(own_table, axis=(3, 4))
    rhs_values = jnp.einsum('strkjv,cstrkj->cstrv', own_table, match_shift, precision=precise)

    def apply_operator(vector):
        own_values = jnp.einsum('strkjv,cstrv->cstrkj', own_table, vector, precision=precise)
        beside = [
            jnp.concatenate([vector[:, :, :, 1:], jnp.zeros_like(vector[:, :, :, :1])], axis=3),
            jnp.concatenate([jnp.zeros_like(vector[:, :, :, :1]), vector[:, :, :, :-1]], axis=3),
            jnp.concatenate([vector[:, :, 1:], jnp.zeros_like(vector[:, :, :1])], axis=2),
            jnp.concatenate([jnp.zeros_like(vector[:, :, :1]), vector[:, :, :-1]], axis=2),
            vector[:, ::-1],
        ]
        partner_values = jnp.stack([jnp.einsum('strjv,cstrv->cstrj', partner_table[:, :, :, number], beside[number], precision=precise) for number in range(5)], axis=4)
        coupling = jnp.einsum('strkjv,cstrkj->cstrv', own_table, own_values - partner_values, precision=precise)
        return anchor_weight * vector + stiffness * (degree * vector - neighbour_sum(vector)) + coupling

    solution = jnp.zeros_like(rhs_values)
    residual = rhs_values
    precond = residual / diagonal
    direction = precond
    norm_now = jnp.sum(residual * precond)
    for iteration in range(ITERS):
        product = apply_operator(direction)
        step_size = norm_now / jnp.sum(direction * product)
        solution = solution + step_size * direction
        residual = residual - step_size * product
        precond = residual / diagonal
        norm_next = jnp.sum(residual * precond)
        direction = precond + (norm_next / norm_now) * direction
        norm_now = norm_next
    return solution, match_shift
```

```python
import functools

import jax
import jax.numpy as jnp
import ml_dtypes
import numpy as np
from jax import lax
from jax.experimental import pallas as pl
from jax.experimental.pallas import tpu as pltpu
from jax.sharding import PartitionSpec as P

P_SIZE = 8
W = 128
V = 32
HALF = W // 2
NV = V * V
GROUP = 4
SLOTS = 128
SECTION = SLOTS // 2
ROWS = 8
EXCHANGES = 4
DOTS = 16

anchor_weight = 0.05
epsilon = 1e-06

BATCHES = ((0, 4), (0, 0), (1, 1), (0, 2), (1, 3))

f32 = jnp.float32
bf16 = jnp.bfloat16
MESH = pl.DeviceIdType.MESH


def split_table(table):
    high = table.astype(ml_dtypes.bfloat16)
    low = (table - high.astype(np.float64)).astype(ml_dtypes.bfloat16)
    return high, low


def tables():
    indices = np.arange(W)
    angles = (indices[:, None] * indices[None, :] % W) * (2.0 * np.pi / W)
    cos, sin = np.cos(angles), np.sin(angles)
    analysis = np.concatenate([cos[:HALF], cos[HALF : HALF + 1], sin[1:HALF]])
    high, low = split_table(analysis)
    first = np.concatenate([high, low], axis=1)
    high, low = split_table(np.block([[cos, sin], [-sin, cos]]))
    middle = np.concatenate([high, high, low], axis=0)
    factors = np.full((W, 1), 2.0)
    factors[0] = factors[HALF] = 1.0
    factors[HALF + 1 :] = -2.0
    high, low = split_table((analysis * factors).T / float(W * W * W))
    last = np.concatenate([high, high, low], axis=1)
    lags = np.where(indices < HALF, indices, np.where(indices == HALF, 0, indices - W))
    lag_rows = np.broadcast_to(lags[:, None], (W, W)).astype(np.float32)
    lag_cols = np.broadcast_to(lags[None, :], (8, W)).astype(np.float32)
    steps = len(BATCHES) * P_SIZE // GROUP
    places = np.zeros((2, steps * 2 * GROUP, SLOTS), np.float32)
    for number, (section, direction) in enumerate(BATCHES):
        for slot in range(P_SIZE):
            step, inner = divmod(number * P_SIZE + slot, GROUP)
            lane = SECTION * section + P_SIZE * direction + slot
            places[0, step * 2 * GROUP + inner, lane] = 1.0
            places[1, step * 2 * GROUP + GROUP + inner, lane] = 1.0
    return first, middle, last, lag_rows, lag_cols, places


def dot(left, right, contract=((1,), (0,))):
    return lax.dot_general(left, right, (contract, ((), ())), preferred_element_type=f32)


def halves(values):
    high = values.astype(bf16)
    low = (values - high.astype(f32)).astype(bf16)
    return high, low


def thirds(values):
    first = values.astype(bf16)
    rest = values - first.astype(f32)
    second = rest.astype(bf16)
    third = (rest - second.astype(f32)).astype(bf16)
    return jnp.concatenate([first, second, third], axis=0)


def join_thirds(values):
    rows = values.shape[0] // 3
    return values[:rows] + (values[rows : 2 * rows] + values[2 * rows :])


def put_first_row(row, block):
    head = block[:8]
    ids = lax.broadcasted_iota(jnp.int32, head.shape, 0)
    return jnp.concatenate([jnp.where(ids == 0, row, head), block[8:]], axis=0)


def correlate(step, own, far, first_ref, middle_ref, last_ref, lag_ref, sums):
    zero_row = jnp.zeros((1, W), f32)
    blocks, own_nyquist, far_nyquist = [], [], []
    for inner in range(GROUP):
        pixels = jnp.concatenate([own[step * GROUP + inner], far[step * GROUP + inner]], axis=1)
        spread = dot(first_ref[...], jnp.concatenate([pixels, pixels], axis=0))
        for lanes, rows in ((0, own_nyquist), (W, far_nyquist)):
            upper = spread[:HALF, lanes : lanes + W]
            lower = spread[HALF:, lanes : lanes + W]
            rows.append(lower[:1])
            blocks.append(jnp.concatenate([upper, put_first_row(zero_row, lower)], axis=1))
    filler = jnp.zeros((8 - GROUP, W), f32)
    nyquist = jnp.concatenate(own_nyquist + [filler] + far_nyquist + [filler], axis=0)
    blocks.append(jnp.concatenate([nyquist, jnp.zeros_like(nyquist)], axis=1))
    high, low = halves(jnp.concatenate(blocks, axis=0))
    spectra = dot(jnp.concatenate([high, low, high], axis=1), middle_ref[...])

    def cross(one, other):
        real = one[:, :W] * other[:, :W] + one[:, W:] * other[:, W:]
        imag = one[:, :W] * other[:, W:] - one[:, W:] * other[:, :W]
        return jnp.concatenate([real, imag], axis=1)

    products = [
        cross(spectra[start : start + HALF], spectra[start + HALF : start + W])
        for start in range(0, GROUP * W, W)
    ]
    start = GROUP * W
    products.append(cross(spectra[start : start + 8], spectra[start + 8 : start + 16]))
    products.append(jnp.zeros((8, 2 * W), f32))
    high, low = halves(jnp.concatenate(products, axis=0))
    waves = dot(jnp.concatenate([high, low, high], axis=1), middle_ref[...])
    columns = []
    for inner in range(GROUP):
        block = waves[inner * HALF : (inner + 1) * HALF]
        row = waves[GROUP * HALF + inner : GROUP * HALF + inner + 1, :W]
        columns.append(
            jnp.concatenate([block[:, :W], put_first_row(row, block[:, W:])], axis=0)
        )
    totals, toward = [], []
    lag = jnp.concatenate([lag_ref[...], lag_ref[...]], axis=1)
    for inner in range(0, GROUP, 2):
        high, low = halves(jnp.concatenate(columns[inner : inner + 2], axis=1))
        surface = dot(last_ref[...], jnp.concatenate([high, low, high], axis=0))
        squared = surface * surface
        weight = squared * squared
        total = jnp.sum(weight, axis=0, keepdims=True)
        moment = jnp.sum(weight * lag, axis=0, keepdims=True)
        totals += [total[:, :W], total[:, W:]]
        toward += [moment[:, :W], moment[:, W:]]
    sums[step] = jnp.concatenate(totals + toward, axis=0)


def kernel(
    nty,
    ntx,
    strips,
    centers,
    lists,
    counts,
    stiffness,
    first_ref,
    middle_ref,
    last_ref,
    lag_rows,
    lag_cols,
    places,
    vertex_out,
    match_out,
    own,
    far,
    sums,
    owner,
    sent,
    received,
    dots_x,
    dots_y,
    local_sem,
    strip_send,
    strip_recv,
    value_send,
    value_recv,
    x_send,
    x_recv,
    y_send,
    y_recv,
):
    ty, tx = lax.axis_index("ty"), lax.axis_index("tx")
    targets = (
        {"ty": ty, "tx": tx - 1},
        {"ty": ty, "tx": tx + 1},
        {"ty": ty - 1, "tx": tx},
        {"ty": ty + 1, "tx": tx},
    )
    west, east, north, south = tx > 0, tx < ntx - 1, ty > 0, ty < nty - 1
    sends = (west, east, north, south)
    receives = (east, west, south, north)

    def patches(ref, batch):
        return ref.at[pl.ds(batch * P_SIZE, P_SIZE)]

    local_copies = [
        pltpu.make_async_copy(source, target, local_sem.at[number])
        for number, (source, target) in enumerate(
            (
                (centers.at[0, 0, 0], patches(own, 0)),
                (centers.at[1, 0, 0], patches(far, 0)),
                (strips.at[0, 0, 0, 0], patches(own, 1)),
                (strips.at[1, 0, 0, 1], patches(far, 2)),
                (strips.at[0, 0, 0, 2], patches(own, 3)),
                (strips.at[1, 0, 0, 3], patches(far, 4)),
            )
        )
    ]
    for copy in local_copies:
        copy.start()
    landing = (patches(far, 1), patches(own, 2), patches(far, 3), patches(own, 4))
    strip_copies = [
        pltpu.make_async_remote_copy(
            src_ref=source,
            dst_ref=landing[number],
            send_sem=strip_send.at[number],
            recv_sem=strip_recv.at[number],
            device_id=targets[number],
            device_id_type=MESH,
        )
        for number, source in enumerate(
            (
                strips.at[0, 0, 0, 1],
                strips.at[1, 0, 0, 0],
                strips.at[0, 0, 0, 3],
                strips.at[1, 0, 0, 2],
            )
        )
    ]
    received[...] = jnp.zeros_like(received)
    for number in range(4):

        @pl.when(jnp.logical_not(receives[number]))
        def _():
            landing[number][...] = jnp.zeros(landing[number].shape, bf16)

    barrier = pltpu.get_barrier_semaphore()
    for offset in range(1, ntx):
        peer = {"ty": ty, "tx": lax.rem(tx + offset, ntx)}
        pl.semaphore_signal(barrier, inc=1, device_id=peer, device_id_type=MESH)
    for offset in range(1, nty):
        peer = {"ty": lax.rem(ty + offset, nty), "tx": tx}
        pl.semaphore_signal(barrier, inc=1, device_id=peer, device_id_type=MESH)
    pl.semaphore_wait(barrier, ntx + nty - 2)

    def start_all(copies):
        for number in range(4):

            @pl.when(sends[number])
            def _():
                copies[number].start()

    def wait_all(copies, numbers):
        for number in numbers:

            @pl.when(receives[number])
            def _():
                copies[number].wait_recv()

    def wait_sent(copies):
        for number in range(4):

            @pl.when(sends[number])
            def _():
                copies[number].wait_send()

    start_all(strip_copies)

    vertex_ids = lax.broadcasted_iota(jnp.int32, (P_SIZE, NV), 1)
    slot_ids = lax.broadcasted_iota(jnp.int32, (P_SIZE, NV), 0)
    groups = []
    for section in range(2):
        for direction in range(5):
            mine = lists[section, 0, 0, direction][:, 0:1]
            used = slot_ids < counts[section, 0, 0, direction]
            groups.append(jnp.where((mine == vertex_ids) & used, 1.0, 0.0))
        groups.append(jnp.zeros((SECTION - 5 * P_SIZE, NV), f32))
    owner[...] = jnp.concatenate(groups, axis=0).astype(bf16)

    def steps(low, high):
        def body(step, carry):
            correlate(step, own, far, first_ref, middle_ref, last_ref, lag_rows, sums)
            return carry

        lax.fori_loop(low, high, body, 0)

    per_batch = P_SIZE // GROUP
    local_copies[0].wait()
    local_copies[1].wait()
    steps(0, per_batch)
    local_copies[2].wait()
    local_copies[3].wait()
    wait_all(strip_copies, (0, 1))
    steps(per_batch, 3 * per_batch)
    local_copies[4].wait()
    local_copies[5].wait()
    wait_all(strip_copies, (2, 3))
    steps(3 * per_batch, 5 * per_batch)

    lanes = lax.broadcasted_iota(jnp.int32, (ROWS, SLOTS), 1)
    rows = lax.broadcasted_iota(jnp.int32, (ROWS, SLOTS), 0)
    direction_ids = lanes % SECTION // P_SIZE
    section_ids = lanes // SECTION
    matching = section_ids == rows // 2 % 2

    def exchange(number, tile):
        sent[number] = tile
        copies = [
            pltpu.make_async_remote_copy(
                src_ref=sent.at[number],
                dst_ref=received.at[number, way],
                send_sem=value_send.at[number, way],
                recv_sem=value_recv.at[number, way],
                device_id=targets[way],
                device_id_type=MESH,
            )
            for way in range(4)
        ]
        start_all(copies)
        partner = pltpu.roll(pltpu.roll(tile, SECTION, 1), 2, 0)
        wait_all(copies, range(4))
        for direction in range(4):
            shift = SLOTS - P_SIZE if direction % 2 == 0 else P_SIZE
            moved = pltpu.roll(received[number, direction], shift, 1)
            partner = jnp.where(direction_ids == direction, moved, partner)
        return copies, partner

    stacked = sums[...].reshape(places.shape[1:])
    plain = jnp.sum(stacked, axis=1, keepdims=True)
    lagged = jnp.sum(stacked * lag_cols[0:1], axis=1, keepdims=True)
    total = jnp.sum(plain * places[0], axis=0, keepdims=True) + epsilon
    toward_cols = jnp.sum(lagged * places[0], axis=0, keepdims=True)
    toward_rows = jnp.sum(plain * places[1], axis=0, keepdims=True)
    offset = jnp.where(rows % 2 == 0, toward_rows / total, toward_cols / total) * (2.0 / W)
    here = (direction_ids == 4) | (direction_ids % 2 == section_ids)
    measured = (here & (direction_ids < 4)) | (here & (section_ids == 0))
    local_shift = jnp.where(section_ids == 0, offset, -offset)
    copies, partner = exchange(0, local_shift)
    pending = [strip_copies, copies]
    shift = jnp.where(measured, local_shift, -partner)
    for component in range(2):
        for section in range(2):
            for direction in range(5):
                lane = SECTION * section + P_SIZE * direction
                row = shift[component : component + 1]
                moved = pltpu.roll(row, SLOTS - lane, 1) if lane else row
                match_out[component, section, 0, 0, direction : direction + 1, :] = moved[
                    :, :P_SIZE
                ]

    def scatter(tile):
        return join_thirds(dot(thirds(jnp.where(matching, tile, 0.0)), owner[...]))

    vertices = lax.broadcasted_iota(jnp.int32, (ROWS, NV), 1)
    column = vertices % V
    left = (column > 0).astype(f32)
    right = (column < V - 1).astype(f32)
    above = (vertices >= V).astype(f32)
    below = (vertices < NV - V).astype(f32)
    field_rows = lax.broadcasted_iota(jnp.int32, (ROWS, NV), 0)
    spring = jnp.where(field_rows // 2 % 2 == 0, stiffness[0, 0, 0], stiffness[1, 0, 0])
    used = dot(jnp.where(matching, 1.0, 0.0).astype(bf16), owner[...])
    diagonal = anchor_weight + spring * (left + right + above + below) + used
    inverse = 1.0 / diagonal

    def smooth(number, field):
        tile = join_thirds(dot(thirds(field), owner[...], ((1,), (1,))))
        copies, partner = exchange(number, tile)
        pending.append(copies)
        around = (
            pltpu.roll(field, 1, 1) * left
            + pltpu.roll(field, NV - 1, 1) * right
            + pltpu.roll(field, V, 1) * above
            + pltpu.roll(field, NV - V, 1) * below
        )
        return (spring * around + scatter(partner)) * inverse

    right_side = scatter(shift)
    base0 = right_side * inverse
    image0 = smooth(1, base0)
    base1 = image0
    image1 = smooth(2, base1)
    base2 = 2.0 * image1 - base0
    image2 = smooth(3, base2)
    bases = (base0, base1, base2)
    applied = tuple(
        diagonal * (base - image) for base, image in zip(bases, (image0, image1, image2))
    )
    pairs = ((0, 0), (0, 1), (0, 2), (1, 1), (1, 2), (2, 2))
    terms = [bases[one] * applied[other] for one, other in pairs]
    terms += [base * right_side for base in bases]
    partial = [jnp.sum(term, axis=0, keepdims=True) for term in terms]
    partial = jnp.concatenate(partial + [jnp.zeros((DOTS - len(terms), NV), f32)], axis=0)
    partial = sum(partial[:, start : start + 128] for start in range(0, NV, 128))

    def all_sum(value, axis, me, count, buffer, send, recv):
        buffer[me] = value
        copies = []
        for offset in range(1, count):
            peer = {"ty": ty, "tx": tx}
            peer[axis] = lax.rem(me + offset, count)
            copy = pltpu.make_async_remote_copy(
                src_ref=buffer.at[me],
                dst_ref=buffer.at[me],
                send_sem=send.at[offset],
                recv_sem=recv.at[offset],
                device_id=peer,
                device_id_type=MESH,
            )
            copy.start()
            copies.append(copy)
        for copy in copies:
            copy.wait_recv()
        total = buffer[0]
        for number in range(1, count):
            total = total + buffer[number]
        return copies, total

    x_copies, partial = all_sum(partial, "tx", tx, ntx, dots_x, x_send, x_recv)
    y_copies, partial = all_sum(partial, "ty", ty, nty, dots_y, y_send, y_recv)
    entries = jnp.sum(partial, axis=1, keepdims=True)
    k00, k01, k02, k11, k12, k22, b0, b1, b2 = (
        entries[number : number + 1] for number in range(len(terms))
    )
    low10, low20 = k01 / k00, k02 / k00
    pivot1 = k11 - low10 * k01
    rest12 = k12 - low10 * k02
    low21 = rest12 / pivot1
    pivot2 = k22 - low20 * k02 - low21 * rest12
    b1 = b1 - low10 * b0
    b2 = b2 - low20 * b0 - low21 * b1
    y2 = b2 / pivot2
    y1 = b1 / pivot1 - low21 * y2
    y0 = b0 / k00 - low10 * y1 - low20 * y2
    result = y0 * base0 + y1 * base1 + y2 * base2
    for component in range(2):
        for section in range(2):
            row = 2 * section + component
            vertex_out[component, section, 0] = result[row : row + 1]

    for copies in pending:
        wait_sent(copies)
    for copy in x_copies + y_copies:
        copy.wait_send()


def local(nty, ntx, strips, centers, match_lists, match_counts, spring_stiffness):
    constants = [jnp.asarray(table) for table in tables()]
    sections = strips.shape[0]
    patches = len(BATCHES) * P_SIZE
    vmem = pl.BlockSpec(memory_space=pltpu.VMEM)
    smem = pl.BlockSpec(memory_space=pltpu.SMEM)
    anywhere = pl.BlockSpec(memory_space=pl.ANY)
    dma = pltpu.SemaphoreType.DMA
    return pl.pallas_call(
        functools.partial(kernel, nty, ntx),
        out_shape=(
            jax.ShapeDtypeStruct((2, sections, 1, 1, NV), f32),
            jax.ShapeDtypeStruct((2, sections, 1, 1, 5, P_SIZE), f32),
        ),
        in_specs=[anywhere, anywhere, vmem, smem, smem] + [vmem] * len(constants),
        out_specs=(vmem, vmem),
        scratch_shapes=[
            pltpu.VMEM((patches, W, W), bf16),
            pltpu.VMEM((patches, W, W), bf16),
            pltpu.VMEM((patches // GROUP, 2 * GROUP, W), f32),
            pltpu.VMEM((SLOTS, NV), bf16),
            pltpu.VMEM((EXCHANGES, ROWS, SLOTS), f32),
            pltpu.VMEM((EXCHANGES, 4, ROWS, SLOTS), f32),
            pltpu.VMEM((ntx, DOTS, 128), f32),
            pltpu.VMEM((nty, DOTS, 128), f32),
            dma((6,)),
            dma((4,)),
            dma((4,)),
            dma((EXCHANGES, 4)),
            dma((EXCHANGES, 4)),
            dma((ntx,)),
            dma((ntx,)),
            dma((nty,)),
            dma((nty,)),
        ],
        compiler_params=pltpu.CompilerParams(
            collective_id=0, has_side_effects=True, vmem_limit_bytes=40 * 1024 * 1024
        ),
    )(strips, centers, match_lists, match_counts, spring_stiffness, *constants)


def solution(mesh):
    return jax.shard_map(
        functools.partial(local, mesh.shape["ty"], mesh.shape["tx"]),
        mesh=mesh,
        in_specs=(
            P(None, "ty", "tx", None, None, None, None),
            P(None, "ty", "tx", None, None, None),
            P(None, "ty", "tx", None, None, None),
            P(None, "ty", "tx", None),
            P(None, "ty", "tx"),
        ),
        out_specs=(P(None, None, "ty", "tx", None), P(None, None, "ty", "tx", None, None)),
        check_vma=False,
    )
```

```python
import functools

import jax
import jax.numpy as jnp
import ml_dtypes
import numpy as np
from jax import lax
from jax.experimental import pallas as pl
from jax.experimental.pallas import tpu as pltpu
from jax.sharding import PartitionSpec as P

P_SIZE = 8
W = 128
V = 32
HALF = W // 2
NV = V * V
GROUP = 4
SLOTS = 128
SECTION = SLOTS // 2
ROWS = 8
EXCHANGES = 3
DOTS = 16

anchor_weight = 0.05
epsilon = 1e-06

BATCHES = ((0, 4), (0, 0), (1, 1), (0, 2), (1, 3))

f32 = jnp.float32
bf16 = jnp.bfloat16
MESH = pl.DeviceIdType.MESH


def split_table(table):
    high = table.astype(ml_dtypes.bfloat16)
    low = (table - high.astype(np.float64)).astype(ml_dtypes.bfloat16)
    return high, low


def tables():
    indices = np.arange(W)
    angles = (indices[:, None] * indices[None, :] % W) * (2.0 * np.pi / W)
    cos, sin = np.cos(angles), np.sin(angles)
    analysis = np.concatenate([cos[:HALF], cos[HALF : HALF + 1], sin[1:HALF]])
    high, low = split_table(analysis)
    first = np.concatenate([high, low], axis=1)
    high, low = split_table(np.block([[cos, sin], [-sin, cos]]))
    middle = np.concatenate([high, high, low], axis=0)
    factors = np.full((W, 1), 2.0)
    factors[0] = factors[HALF] = 1.0
    factors[HALF + 1 :] = -2.0
    high, low = split_table((analysis * factors).T / float(W * W * W))
    last = np.concatenate([high, high, low], axis=1)
    return first, middle, last


def lag_values(shape, dimension):
    ids = lax.broadcasted_iota(jnp.int32, shape, dimension)
    lags = jnp.where(ids < HALF, ids, jnp.where(ids == HALF, 0, ids - W))
    return lags.astype(f32)


def dot(left, right, contract=((1,), (0,))):
    return lax.dot_general(left, right, (contract, ((), ())), preferred_element_type=f32)


def halves(values):
    high = values.astype(bf16)
    low = (values - high.astype(f32)).astype(bf16)
    return high, low


def thirds(values):
    first = values.astype(bf16)
    rest = values - first.astype(f32)
    second = rest.astype(bf16)
    third = (rest - second.astype(f32)).astype(bf16)
    return jnp.concatenate([first, second, third], axis=0)


def join_thirds(values):
    rows = values.shape[0] // 3
    return values[:rows] + (values[rows : 2 * rows] + values[2 * rows :])


def put_first_row(row, block):
    head = block[:8]
    ids = lax.broadcasted_iota(jnp.int32, head.shape, 0)
    return jnp.concatenate([jnp.where(ids == 0, row, head), block[8:]], axis=0)


def correlate(step, own, far, first_ref, middle_ref, last_ref, lag_ref, sums):
    zero_row = jnp.zeros((1, W), f32)
    blocks, own_nyquist, far_nyquist = [], [], []
    for inner in range(GROUP):
        pixels = jnp.concatenate([own[step * GROUP + inner], far[step * GROUP + inner]], axis=1)
        spread = dot(first_ref[...], jnp.concatenate([pixels, pixels], axis=0))
        for lanes, rows in ((0, own_nyquist), (W, far_nyquist)):
            upper = spread[:HALF, lanes : lanes + W]
            lower = spread[HALF:, lanes : lanes + W]
            rows.append(lower[:1])
            blocks.append(jnp.concatenate([upper, put_first_row(zero_row, lower)], axis=1))
    filler = jnp.zeros((8 - GROUP, W), f32)
    nyquist = jnp.concatenate(own_nyquist + [filler] + far_nyquist + [filler], axis=0)
    blocks.append(jnp.concatenate([nyquist, jnp.zeros_like(nyquist)], axis=1))
    high, low = halves(jnp.concatenate(blocks, axis=0))
    spectra = dot(jnp.concatenate([high, low, high], axis=1), middle_ref[...])

    def cross(one, other):
        real = one[:, :W] * other[:, :W] + one[:, W:] * other[:, W:]
        imag = one[:, :W] * other[:, W:] - one[:, W:] * other[:, :W]
        return jnp.concatenate([real, imag], axis=1)

    products = [
        cross(spectra[start : start + HALF], spectra[start + HALF : start + W])
        for start in range(0, GROUP * W, W)
    ]
    start = GROUP * W
    products.append(cross(spectra[start : start + 8], spectra[start + 8 : start + 16]))
    products.append(jnp.zeros((8, 2 * W), f32))
    high, low = halves(jnp.concatenate(products, axis=0))
    waves = dot(jnp.concatenate([high, low, high], axis=1), middle_ref[...])
    columns = []
    for inner in range(GROUP):
        block = waves[inner * HALF : (inner + 1) * HALF]
        row = waves[GROUP * HALF + inner : GROUP * HALF + inner + 1, :W]
        columns.append(
            jnp.concatenate([block[:, :W], put_first_row(row, block[:, W:])], axis=0)
        )
    totals, toward = [], []
    lag = lag_ref[...]
    for inner in range(0, GROUP, 2):
        high, low = halves(jnp.concatenate(columns[inner : inner + 2], axis=1))
        surface = dot(last_ref[...], jnp.concatenate([high, low, high], axis=0))
        squared = surface * surface
        weight = squared * squared
        total = jnp.sum(weight, axis=0, keepdims=True)
        moment = jnp.sum(weight * lag, axis=0, keepdims=True)
        totals += [total[:, :W], total[:, W:]]
        toward += [moment[:, :W], moment[:, W:]]
    sums[step] = jnp.concatenate(totals + toward, axis=0)


def kernel(
    nty,
    ntx,
    strips,
    centers,
    lists_in,
    counts_in,
    stiffness_in,
    first_in,
    middle_in,
    last_in,
    vertex_out,
    match_out,
    lists,
    counts,
    stiffness,
    first_ref,
    middle_ref,
    last_ref,
    lag_rows,
    owner_t,
    own,
    far,
    sums,
    owner,
    sent,
    received,
    dots_x,
    dots_y,
    local_sem,
    strip_send,
    strip_recv,
    value_send,
    value_recv,
    x_send,
    x_recv,
    y_send,
    y_recv,
):
    ty, tx = lax.axis_index("ty"), lax.axis_index("tx")
    targets = (
        {"ty": ty, "tx": tx - 1},
        {"ty": ty, "tx": tx + 1},
        {"ty": ty - 1, "tx": tx},
        {"ty": ty + 1, "tx": tx},
    )
    west, east, north, south = tx > 0, tx < ntx - 1, ty > 0, ty < nty - 1
    sends = (west, east, north, south)
    receives = (east, west, south, north)

    def patches(ref, batch):
        return ref.at[pl.ds(batch * P_SIZE, P_SIZE)]

    local_copies = [
        pltpu.make_async_copy(source, target, local_sem.at[number])
        for number, (source, target) in enumerate(
            (
                (centers.at[0, 0, 0], patches(own, 0)),
                (centers.at[1, 0, 0], patches(far, 0)),
                (strips.at[0, 0, 0, 0], patches(own, 1)),
                (strips.at[1, 0, 0, 1], patches(far, 2)),
                (strips.at[0, 0, 0, 2], patches(own, 3)),
                (strips.at[1, 0, 0, 3], patches(far, 4)),
                (first_in, first_ref),
                (middle_in, middle_ref),
                (last_in, last_ref),
                (lists_in, lists),
                (counts_in, counts),
                (stiffness_in, stiffness),
            )
        )
    ]
    for copy in local_copies:
        copy.start()
    landing = (patches(far, 1), patches(own, 2), patches(far, 3), patches(own, 4))
    strip_copies = [
        pltpu.make_async_remote_copy(
            src_ref=source,
            dst_ref=landing[number],
            send_sem=strip_send.at[number],
            recv_sem=strip_recv.at[number],
            device_id=targets[number],
            device_id_type=MESH,
        )
        for number, source in enumerate(
            (
                strips.at[0, 0, 0, 1],
                strips.at[1, 0, 0, 0],
                strips.at[0, 0, 0, 3],
                strips.at[1, 0, 0, 2],
            )
        )
    ]
    received[...] = jnp.zeros_like(received)
    for number in range(4):

        @pl.when(jnp.logical_not(receives[number]))
        def _():
            landing[number][...] = jnp.zeros(landing[number].shape, bf16)

    barrier = pltpu.get_barrier_semaphore()
    for offset in range(1, ntx):
        peer = {"ty": ty, "tx": lax.rem(tx + offset, ntx)}
        pl.semaphore_signal(barrier, inc=1, device_id=peer, device_id_type=MESH)
    for offset in range(1, nty):
        peer = {"ty": lax.rem(ty + offset, nty), "tx": tx}
        pl.semaphore_signal(barrier, inc=1, device_id=peer, device_id_type=MESH)
    pl.semaphore_wait(barrier, ntx + nty - 2)

    def start_all(copies):
        for number in range(4):

            @pl.when(sends[number])
            def _():
                copies[number].start()

    def wait_all(copies, numbers):
        for number in numbers:

            @pl.when(receives[number])
            def _():
                copies[number].wait_recv()

    def wait_sent(copies):
        for number in range(4):

            @pl.when(sends[number])
            def _():
                copies[number].wait_send()

    start_all(strip_copies)

    for copy in local_copies[6:]:
        copy.wait()
    lag_rows[...] = lag_values((W, 2 * W), 0)
    lanes = lax.broadcasted_iota(jnp.int32, (ROWS, SLOTS), 1)
    rows = lax.broadcasted_iota(jnp.int32, (ROWS, SLOTS), 0)
    direction_ids = lanes % SECTION // P_SIZE
    section_ids = lanes // SECTION
    matching = section_ids == rows // 2 % 2
    mine, limit = [], jnp.zeros((1, SLOTS), jnp.int32)
    for section in range(2):
        for direction in range(5):
            mine.append(lists[section, 0, 0, direction, 0:1, :])
            inside = (direction_ids[:1] == direction) & (section_ids[:1] == section)
            limit = jnp.where(inside, counts[section, 0, 0, direction], limit)
        mine.append(jnp.zeros((1, SECTION - 5 * P_SIZE), jnp.int32))
    mine = jnp.concatenate(mine, axis=1)
    mine = jnp.where(lanes[:1] % P_SIZE < limit, mine, -1)
    owner_t[...] = jnp.where(
        lax.broadcasted_iota(jnp.int32, (NV, SLOTS), 0) == mine, 1.0, 0.0
    ).astype(bf16)
    square = (SLOTS, SLOTS)
    same = lax.broadcasted_iota(jnp.int32, square, 0) == lax.broadcasted_iota(jnp.int32, square, 1)
    turned = jnp.sum(jnp.where(same, mine.astype(f32), 0.0), axis=1, keepdims=True)
    owner[...] = jnp.where(
        lax.broadcasted_iota(jnp.int32, (SLOTS, NV), 1) == turned.astype(jnp.int32), 1.0, 0.0
    ).astype(bf16)

    def steps(low, high):
        def body(step, carry):
            correlate(step, own, far, first_ref, middle_ref, last_ref, lag_rows, sums)
            return carry

        lax.fori_loop(low, high, body, 0)

    per_batch = P_SIZE // GROUP
    local_copies[0].wait()
    local_copies[1].wait()
    steps(0, per_batch)
    local_copies[2].wait()
    local_copies[3].wait()
    wait_all(strip_copies, (0, 1))
    steps(per_batch, 3 * per_batch)
    local_copies[4].wait()
    local_copies[5].wait()
    wait_all(strip_copies, (2, 3))
    steps(3 * per_batch, 5 * per_batch)

    def exchange(number, tile):
        sent[number] = tile
        copies = [
            pltpu.make_async_remote_copy(
                src_ref=sent.at[number],
                dst_ref=received.at[number, way],
                send_sem=value_send.at[number, way],
                recv_sem=value_recv.at[number, way],
                device_id=targets[way],
                device_id_type=MESH,
            )
            for way in range(4)
        ]
        start_all(copies)
        partner = pltpu.roll(pltpu.roll(tile, SECTION, 1), 2, 0)
        wait_all(copies, range(4))
        for direction in range(4):
            shift = SLOTS - P_SIZE if direction % 2 == 0 else P_SIZE
            moved = pltpu.roll(received[number, direction], shift, 1)
            partner = jnp.where(direction_ids == direction, moved, partner)
        return copies, partner

    shape = (sums.shape[0] * sums.shape[1], SLOTS)
    stacked = sums[...].reshape(shape)
    row_ids = lax.broadcasted_iota(jnp.int32, shape, 0)
    step_ids, inner_ids = row_ids // (2 * GROUP), row_ids % (2 * GROUP)
    batch_ids = step_ids // per_batch
    first_lane = jnp.zeros(shape, jnp.int32)
    for number, (section, direction) in enumerate(BATCHES):
        lane = SECTION * section + P_SIZE * direction
        first_lane = jnp.where(batch_ids == number, lane, first_lane)
    place = first_lane + step_ids % per_batch * GROUP + inner_ids % GROUP
    placed = place == lax.broadcasted_iota(jnp.int32, shape, 1)
    is_total = placed & (inner_ids < GROUP)
    is_moment = placed & (inner_ids >= GROUP)
    plain = jnp.sum(stacked, axis=1, keepdims=True)
    lagged = jnp.sum(stacked * lag_values((1, W), 1), axis=1, keepdims=True)
    total = jnp.sum(jnp.where(is_total, plain, 0.0), axis=0, keepdims=True) + epsilon
    toward_cols = jnp.sum(jnp.where(is_total, lagged, 0.0), axis=0, keepdims=True)
    toward_rows = jnp.sum(jnp.where(is_moment, plain, 0.0), axis=0, keepdims=True)
    offset = jnp.where(rows % 2 == 0, toward_rows / total, toward_cols / total) * (2.0 / W)
    here = (direction_ids == 4) | (direction_ids % 2 == section_ids)
    measured = (here & (direction_ids < 4)) | (here & (section_ids == 0))
    local_shift = jnp.where(section_ids == 0, offset, -offset)
    copies, partner = exchange(0, local_shift)
    pending = [strip_copies, copies]
    shift = jnp.where(measured, local_shift, -partner)
    for component in range(2):
        for section in range(2):
            for direction in range(5):
                lane = SECTION * section + P_SIZE * direction
                row = shift[component : component + 1]
                moved = pltpu.roll(row, SLOTS - lane, 1) if lane else row
                match_out[component, section, 0, direction] = moved[:, :P_SIZE]

    def scatter(tile):
        return join_thirds(dot(thirds(jnp.where(matching, tile, 0.0)), owner[...]))

    vertices = lax.broadcasted_iota(jnp.int32, (ROWS, NV), 1)
    column = vertices % V
    left = (column > 0).astype(f32)
    right = (column < V - 1).astype(f32)
    above = (vertices >= V).astype(f32)
    below = (vertices < NV - V).astype(f32)
    field_rows = lax.broadcasted_iota(jnp.int32, (ROWS, NV), 0)
    spring = jnp.where(field_rows // 2 % 2 == 0, stiffness[0, 0, 0], stiffness[0, 0, 1])
    used = dot(jnp.where(matching, 1.0, 0.0).astype(bf16), owner[...])
    diagonal = anchor_weight + spring * (left + right + above + below) + used
    inverse = 1.0 / diagonal

    def gather(field):
        return join_thirds(dot(thirds(field), owner_t[...]))

    def around(field):
        return spring * (
            pltpu.roll(field, 1, 1) * left
            + pltpu.roll(field, NV - 1, 1) * right
            + pltpu.roll(field, V, 1) * above
            + pltpu.roll(field, NV - V, 1) * below
        )

    def smooth(number, field):
        copies, partner = exchange(number, gather(field))
        pending.append(copies)
        return (around(field) + scatter(partner)) * inverse

    right_side = scatter(shift)
    base0 = right_side * inverse
    image0 = smooth(1, base0)
    base1 = image0
    image1 = smooth(2, base1)
    base2 = 2.0 * image1 - base0
    bases = (base0, base1, base2)
    applied = (
        diagonal * (base0 - image0),
        diagonal * (base1 - image1),
        diagonal * base2 - around(base2),
    )
    pairs = ((0, 0), (0, 1), (0, 2), (1, 1), (1, 2), (2, 2))
    terms = [applied[one] * bases[other] for one, other in pairs]
    terms += [base * right_side for base in bases]
    partial = jnp.concatenate([jnp.sum(term, axis=0, keepdims=True) for term in terms], axis=0)
    partial = sum(partial[:, start : start + SLOTS] for start in range(0, NV, SLOTS))
    tile = gather(base2)
    values = jnp.where(section_ids[:2] == 0, tile[:2], tile[2:4])
    filler = jnp.zeros((DOTS - len(terms) - 2, SLOTS), f32)
    partial = jnp.concatenate([partial, values, filler], axis=0)
    last = pairs.index((2, 2))

    def couple(entries, low, high, direction, reach):
        product = jnp.where(direction_ids[:1] == direction, low * pltpu.roll(high, reach, 1), 0.0)
        product = 4.0 * jnp.sum(product, axis=0, keepdims=True)
        ids = lax.broadcasted_iota(jnp.int32, entries.shape, 0)
        return entries - jnp.where(ids == last, product, 0.0)

    cross = jnp.where(section_ids[:1] == 0, values, 0.0)
    partial = couple(partial, cross, values, 4, SECTION)

    def all_sum(value, axis, me, count, buffer, send, recv):
        buffer[me] = value
        copies = []
        for offset in range(1, count):
            peer = {"ty": ty, "tx": tx}
            peer[axis] = lax.rem(me + offset, count)
            copy = pltpu.make_async_remote_copy(
                src_ref=buffer.at[me],
                dst_ref=buffer.at[me],
                send_sem=send.at[offset],
                recv_sem=recv.at[offset],
                device_id=peer,
                device_id_type=MESH,
            )
            copy.start()
            copies.append(copy)
        for copy in copies:
            copy.wait_recv()
        total = buffer[0, :DOTS]
        for number in range(1, count):
            total = total + buffer[number, :DOTS]
        return copies, total

    x_copies, partial = all_sum(partial, "tx", tx, ntx, dots_x, x_send, x_recv)
    start = len(terms)
    values = [dots_x[number, start : start + 2] for number in range(ntx)]
    held = jnp.concatenate(values, axis=0)
    if ntx > 1:
        partial = couple(partial, held[:-2], held[2:], 0, SLOTS - P_SIZE)
    missing = dots_y.shape[1] - DOTS - 2 * ntx
    filler = [jnp.zeros((missing, SLOTS), f32)] if missing else []
    tall = jnp.concatenate([partial, held] + filler, axis=0)
    y_copies, partial = all_sum(tall, "ty", ty, nty, dots_y, y_send, y_recv)
    for number in range(nty - 1):
        partial = couple(
            partial, dots_y[number, DOTS:], dots_y[number + 1, DOTS:], 2, SLOTS - P_SIZE
        )
    entries = jnp.sum(partial, axis=1, keepdims=True)
    k00, k01, k02, k11, k12, k22, b0, b1, b2 = (
        entries[number : number + 1] for number in range(len(terms))
    )
    low10, low20 = k01 / k00, k02 / k00
    pivot1 = k11 - low10 * k01
    rest12 = k12 - low10 * k02
    low21 = rest12 / pivot1
    pivot2 = k22 - low20 * k02 - low21 * rest12
    b1 = b1 - low10 * b0
    b2 = b2 - low20 * b0 - low21 * b1
    y2 = b2 / pivot2
    y1 = b1 / pivot1 - low21 * y2
    y0 = b0 / k00 - low10 * y1 - low20 * y2
    result = y0 * base0 + y1 * base1 + y2 * base2
    for component in range(2):
        for section in range(2):
            row = 2 * section + component
            vertex_out[component, section, 0] = result[row : row + 1]

    for copies in pending:
        wait_sent(copies)
    for copy in x_copies + y_copies:
        copy.wait_send()


def local(nty, ntx, strips, centers, match_lists, match_counts, spring_stiffness):
    constants = [jnp.asarray(table) for table in tables()]
    sections = strips.shape[0]
    patches = len(BATCHES) * P_SIZE
    vmem = pl.BlockSpec(memory_space=pltpu.VMEM)
    hbm = pl.BlockSpec(memory_space=pltpu.HBM)
    dma = pltpu.SemaphoreType.DMA
    match_lists = jnp.swapaxes(match_lists, 4, 5)
    spring_stiffness = spring_stiffness.transpose(1, 2, 0)
    operands = (strips, centers, match_lists, match_counts, spring_stiffness, *constants)
    tall = DOTS + -(-2 * ntx // 8) * 8
    vertex_shift, match_shift = pl.pallas_call(
        functools.partial(kernel, nty, ntx),
        out_shape=(
            jax.ShapeDtypeStruct((2, sections, 1, 1, NV), f32),
            jax.ShapeDtypeStruct((2, sections, 1, 5, 1, P_SIZE), f32),
        ),
        in_specs=[hbm] * len(operands),
        out_specs=(vmem, vmem),
        scratch_shapes=[
            pltpu.VMEM(match_lists.shape, jnp.int32),
            pltpu.SMEM(match_counts.shape, jnp.int32),
            pltpu.SMEM(spring_stiffness.shape, f32),
            *[pltpu.VMEM(table.shape, bf16) for table in constants],
            pltpu.VMEM((W, 2 * W), f32),
            pltpu.VMEM((NV, SLOTS), bf16),
            pltpu.VMEM((patches, W, W), bf16),
            pltpu.VMEM((patches, W, W), bf16),
            pltpu.VMEM((patches // GROUP, 2 * GROUP, W), f32),
            pltpu.VMEM((SLOTS, NV), bf16),
            pltpu.VMEM((EXCHANGES, ROWS, SLOTS), f32),
            pltpu.VMEM((EXCHANGES, 4, ROWS, SLOTS), f32),
            pltpu.VMEM((ntx, DOTS, SLOTS), f32),
            pltpu.VMEM((nty, tall, SLOTS), f32),
            dma((12,)),
            dma((4,)),
            dma((4,)),
            dma((EXCHANGES, 4)),
            dma((EXCHANGES, 4)),
            dma((ntx,)),
            dma((ntx,)),
            dma((nty,)),
            dma((nty,)),
        ],
        compiler_params=pltpu.CompilerParams(
            collective_id=0, has_side_effects=True, vmem_limit_bytes=63 * 1024 * 1024
        ),
    )(*operands)
    return vertex_shift, jnp.swapaxes(match_shift, 3, 4)


def solution(mesh):
    return jax.shard_map(
        functools.partial(local, mesh.shape["ty"], mesh.shape["tx"]),
        mesh=mesh,
        in_specs=(
            P(None, "ty", "tx", None, None, None, None),
            P(None, "ty", "tx", None, None, None),
            P(None, "ty", "tx", None, None, None),
            P(None, "ty", "tx", None),
            P(None, "ty", "tx"),
        ),
        out_specs=(P(None, None, "ty", "tx", None), P(None, None, "ty", "tx", None, None)),
        check_vma=False,
    )
```

```python
import functools

import jax
import jax.numpy as jnp
import ml_dtypes
import numpy as np
from jax import lax
from jax.experimental import pallas as pl
from jax.experimental.pallas import tpu as pltpu
from jax.sharding import PartitionSpec as P

P_SIZE = 8
W = 128
V = 32
HALF = W // 2
NV = V * V
GROUP = 4
SLOTS = 128
SECTION = SLOTS // 2
ROWS = 8
EXCHANGES = 3
DOTS = 16

anchor_weight = 0.05
epsilon = 1e-06

BATCHES = ((0, 4), (0, 0), (1, 1), (0, 2), (1, 3))

f32 = jnp.float32
bf16 = jnp.bfloat16
MESH = pl.DeviceIdType.MESH


def split_table(table):
    high = table.astype(ml_dtypes.bfloat16)
    low = (table - high.astype(np.float64)).astype(ml_dtypes.bfloat16)
    return high, low


def tables():
    indices = np.arange(W)
    angles = (indices[:, None] * indices[None, :] % W) * (2.0 * np.pi / W)
    cos, sin = np.cos(angles), np.sin(angles)
    analysis = np.concatenate([cos[:HALF], cos[HALF : HALF + 1], sin[1:HALF]])
    high, low = split_table(analysis)
    first = np.concatenate([high, low], axis=1)
    high, low = split_table(np.block([[cos, sin], [-sin, cos]]))
    middle = np.concatenate([high, high, low], axis=0)
    factors = np.full((W, 1), 2.0)
    factors[0] = factors[HALF] = 1.0
    factors[HALF + 1 :] = -2.0
    high, low = split_table((analysis * factors).T / float(W * W * W))
    last = np.concatenate([high, high, low], axis=1)
    return first, middle, last


def lag_values(shape, dimension):
    ids = lax.broadcasted_iota(jnp.int32, shape, dimension)
    lags = jnp.where(ids < HALF, ids, jnp.where(ids == HALF, 0, ids - W))
    return lags.astype(f32)


def dot(left, right, contract=((1,), (0,))):
    return lax.dot_general(left, right, (contract, ((), ())), preferred_element_type=f32)


def halves(values):
    high = values.astype(bf16)
    low = (values - high.astype(f32)).astype(bf16)
    return high, low


def thirds(values):
    first = values.astype(bf16)
    rest = values - first.astype(f32)
    second = rest.astype(bf16)
    third = (rest - second.astype(f32)).astype(bf16)
    return jnp.concatenate([first, second, third], axis=0)


def join_thirds(values):
    rows = values.shape[0] // 3
    return values[:rows] + (values[rows : 2 * rows] + values[2 * rows :])


def put_first_row(row, block):
    head = block[:8]
    ids = lax.broadcasted_iota(jnp.int32, head.shape, 0)
    return jnp.concatenate([jnp.where(ids == 0, row, head), block[8:]], axis=0)


def analyse(step, own, far, first_ref, middle_ref):
    zero_row = jnp.zeros((1, W), f32)
    blocks, own_nyquist, far_nyquist = [], [], []
    for inner in range(GROUP):
        pixels = jnp.concatenate([own[step * GROUP + inner], far[step * GROUP + inner]], axis=1)
        spread = dot(first_ref[...], jnp.concatenate([pixels, pixels], axis=0))
        for lanes, rows in ((0, own_nyquist), (W, far_nyquist)):
            upper = spread[:HALF, lanes : lanes + W]
            lower = spread[HALF:, lanes : lanes + W]
            rows.append(lower[:1])
            blocks.append(jnp.concatenate([upper, put_first_row(zero_row, lower)], axis=1))
    filler = jnp.zeros((8 - GROUP, W), f32)
    nyquist = jnp.concatenate(own_nyquist + [filler] + far_nyquist + [filler], axis=0)
    blocks.append(jnp.concatenate([nyquist, jnp.zeros_like(nyquist)], axis=1))
    high, low = halves(jnp.concatenate(blocks, axis=0))
    spectra = dot(jnp.concatenate([high, low, high], axis=1), middle_ref[...])

    def cross(one, other):
        real = one[:, :W] * other[:, :W] + one[:, W:] * other[:, W:]
        imag = one[:, :W] * other[:, W:] - one[:, W:] * other[:, :W]
        return jnp.concatenate([real, imag], axis=1)

    products = [
        cross(spectra[start : start + HALF], spectra[start + HALF : start + W])
        for start in range(0, GROUP * W, W)
    ]
    start = GROUP * W
    products.append(cross(spectra[start : start + 8], spectra[start + 8 : start + 16]))
    products.append(jnp.zeros((8, 2 * W), f32))
    return halves(jnp.concatenate(products, axis=0))


def synthesise(step, products, middle_ref, last_ref, lag_ref, sums):
    high, low = products
    waves = dot(jnp.concatenate([high, low, high], axis=1), middle_ref[...])
    columns = []
    for inner in range(GROUP):
        block = waves[inner * HALF : (inner + 1) * HALF]
        row = waves[GROUP * HALF + inner : GROUP * HALF + inner + 1, :W]
        columns.append(
            jnp.concatenate([block[:, :W], put_first_row(row, block[:, W:])], axis=0)
        )
    totals, toward = [], []
    lag = lag_ref[...]
    for inner in range(0, GROUP, 2):
        high, low = halves(jnp.concatenate(columns[inner : inner + 2], axis=1))
        surface = dot(last_ref[...], jnp.concatenate([high, low, high], axis=0))
        squared = surface * surface
        weight = squared * squared
        total = jnp.sum(weight, axis=0, keepdims=True)
        moment = jnp.sum(weight * lag, axis=0, keepdims=True)
        totals += [total[:, :W], total[:, W:]]
        toward += [moment[:, :W], moment[:, W:]]
    sums[step] = jnp.concatenate(totals + toward, axis=0)


def kernel(
    nty,
    ntx,
    strips,
    centers,
    lists_in,
    counts_in,
    stiffness_in,
    first_in,
    middle_in,
    last_in,
    vertex_out,
    match_out,
    lists,
    counts,
    stiffness,
    first_ref,
    middle_ref,
    last_ref,
    lag_rows,
    owner_t,
    own,
    far,
    sums,
    owner,
    sent,
    received,
    dots_x,
    dots_y,
    local_sem,
    strip_send,
    strip_recv,
    value_send,
    value_recv,
    x_send,
    x_recv,
    y_send,
    y_recv,
):
    ty, tx = lax.axis_index("ty"), lax.axis_index("tx")
    targets = (
        {"ty": ty, "tx": tx - 1},
        {"ty": ty, "tx": tx + 1},
        {"ty": ty - 1, "tx": tx},
        {"ty": ty + 1, "tx": tx},
    )
    west, east, north, south = tx > 0, tx < ntx - 1, ty > 0, ty < nty - 1
    sends = (west, east, north, south)
    receives = (east, west, south, north)

    def patches(ref, batch):
        return ref.at[pl.ds(batch * P_SIZE, P_SIZE)]

    local_copies = [
        pltpu.make_async_copy(source, target, local_sem.at[number])
        for number, (source, target) in enumerate(
            (
                (centers.at[0, 0, 0], patches(own, 0)),
                (centers.at[1, 0, 0], patches(far, 0)),
                (strips.at[0, 0, 0, 0], patches(own, 1)),
                (strips.at[1, 0, 0, 1], patches(far, 2)),
                (strips.at[0, 0, 0, 2], patches(own, 3)),
                (strips.at[1, 0, 0, 3], patches(far, 4)),
                (first_in, first_ref),
                (middle_in, middle_ref),
                (last_in, last_ref),
                (lists_in, lists),
                (counts_in, counts),
                (stiffness_in, stiffness),
            )
        )
    ]
    for copy in local_copies:
        copy.start()
    landing = (patches(far, 1), patches(own, 2), patches(far, 3), patches(own, 4))
    strip_copies = [
        pltpu.make_async_remote_copy(
            src_ref=source,
            dst_ref=landing[number],
            send_sem=strip_send.at[number],
            recv_sem=strip_recv.at[number],
            device_id=targets[number],
            device_id_type=MESH,
        )
        for number, source in enumerate(
            (
                strips.at[0, 0, 0, 1],
                strips.at[1, 0, 0, 0],
                strips.at[0, 0, 0, 3],
                strips.at[1, 0, 0, 2],
            )
        )
    ]
    received[...] = jnp.zeros_like(received)
    for number in range(4):

        @pl.when(jnp.logical_not(receives[number]))
        def _():
            landing[number][...] = jnp.zeros(landing[number].shape, bf16)

    barrier = pltpu.get_barrier_semaphore()
    for offset in range(1, ntx):
        peer = {"ty": ty, "tx": lax.rem(tx + offset, ntx)}
        pl.semaphore_signal(barrier, inc=1, device_id=peer, device_id_type=MESH)
    for offset in range(1, nty):
        peer = {"ty": lax.rem(ty + offset, nty), "tx": tx}
        pl.semaphore_signal(barrier, inc=1, device_id=peer, device_id_type=MESH)
    pl.semaphore_wait(barrier, ntx + nty - 2)

    def start_all(copies):
        for number in range(4):

            @pl.when(sends[number])
            def _():
                copies[number].start()

    def wait_all(copies, numbers):
        for number in numbers:

            @pl.when(receives[number])
            def _():
                copies[number].wait_recv()

    def wait_sent(copies):
        for number in range(4):

            @pl.when(sends[number])
            def _():
                copies[number].wait_send()

    start_all(strip_copies)

    for copy in local_copies[6:]:
        copy.wait()
    lag_rows[...] = lag_values((W, 2 * W), 0)
    lanes = lax.broadcasted_iota(jnp.int32, (ROWS, SLOTS), 1)
    rows = lax.broadcasted_iota(jnp.int32, (ROWS, SLOTS), 0)
    direction_ids = lanes % SECTION // P_SIZE
    section_ids = lanes // SECTION
    matching = section_ids == rows // 2 % 2
    mine, limit = [], jnp.zeros((1, SLOTS), jnp.int32)
    for section in range(2):
        for direction in range(5):
            mine.append(lists[section, 0, 0, direction, 0:1, :])
            inside = (direction_ids[:1] == direction) & (section_ids[:1] == section)
            limit = jnp.where(inside, counts[section, 0, 0, direction], limit)
        mine.append(jnp.zeros((1, SECTION - 5 * P_SIZE), jnp.int32))
    mine = jnp.concatenate(mine, axis=1)
    mine = jnp.where(lanes[:1] % P_SIZE < limit, mine, -1)
    owner_t[...] = jnp.where(
        lax.broadcasted_iota(jnp.int32, (NV, SLOTS), 0) == mine, 1.0, 0.0
    ).astype(bf16)
    square = (SLOTS, SLOTS)
    same = lax.broadcasted_iota(jnp.int32, square, 0) == lax.broadcasted_iota(jnp.int32, square, 1)
    turned = jnp.sum(jnp.where(same, mine.astype(f32), 0.0), axis=1, keepdims=True)
    owner[...] = jnp.where(
        lax.broadcasted_iota(jnp.int32, (SLOTS, NV), 1) == turned.astype(jnp.int32), 1.0, 0.0
    ).astype(bf16)

    def analysis(step):
        return analyse(step, own, far, first_ref, middle_ref)

    def synthesis(step, products):
        synthesise(step, products, middle_ref, last_ref, lag_rows, sums)

    def steps(low, high, products):
        def body(step, held):
            fresh = analysis(step + 1)
            synthesis(step, held)
            return fresh

        return lax.fori_loop(low, high, body, products)

    per_batch = P_SIZE // GROUP
    count = len(BATCHES) * per_batch
    local_copies[0].wait()
    local_copies[1].wait()
    products = steps(0, per_batch - 1, analysis(0))
    local_copies[2].wait()
    local_copies[3].wait()
    wait_all(strip_copies, (0, 1))
    products = steps(per_batch - 1, 3 * per_batch - 1, products)
    local_copies[4].wait()
    local_copies[5].wait()
    wait_all(strip_copies, (2, 3))
    products = steps(3 * per_batch - 1, count - 1, products)
    synthesis(count - 1, products)

    def exchange(number, tile):
        sent[number] = tile
        copies = [
            pltpu.make_async_remote_copy(
                src_ref=sent.at[number],
                dst_ref=received.at[number, way],
                send_sem=value_send.at[number, way],
                recv_sem=value_recv.at[number, way],
                device_id=targets[way],
                device_id_type=MESH,
            )
            for way in range(4)
        ]
        start_all(copies)
        partner = pltpu.roll(pltpu.roll(tile, SECTION, 1), 2, 0)
        wait_all(copies, range(4))
        for direction in range(4):
            shift = SLOTS - P_SIZE if direction % 2 == 0 else P_SIZE
            moved = pltpu.roll(received[number, direction], shift, 1)
            partner = jnp.where(direction_ids == direction, moved, partner)
        return copies, partner

    shape = (sums.shape[0] * sums.shape[1], SLOTS)
    stacked = sums[...].reshape(shape)
    row_ids = lax.broadcasted_iota(jnp.int32, shape, 0)
    step_ids, inner_ids = row_ids // (2 * GROUP), row_ids % (2 * GROUP)
    batch_ids = step_ids // per_batch
    first_lane = jnp.zeros(shape, jnp.int32)
    for number, (section, direction) in enumerate(BATCHES):
        lane = SECTION * section + P_SIZE * direction
        first_lane = jnp.where(batch_ids == number, lane, first_lane)
    place = first_lane + step_ids % per_batch * GROUP + inner_ids % GROUP
    placed = place == lax.broadcasted_iota(jnp.int32, shape, 1)
    is_total = placed & (inner_ids < GROUP)
    is_moment = placed & (inner_ids >= GROUP)
    plain = jnp.sum(stacked, axis=1, keepdims=True)
    lagged = jnp.sum(stacked * lag_values((1, W), 1), axis=1, keepdims=True)
    total = jnp.sum(jnp.where(is_total, plain, 0.0), axis=0, keepdims=True) + epsilon
    toward_cols = jnp.sum(jnp.where(is_total, lagged, 0.0), axis=0, keepdims=True)
    toward_rows = jnp.sum(jnp.where(is_moment, plain, 0.0), axis=0, keepdims=True)
    offset = jnp.where(rows % 2 == 0, toward_rows / total, toward_cols / total) * (2.0 / W)
    here = (direction_ids == 4) | (direction_ids % 2 == section_ids)
    measured = (here & (direction_ids < 4)) | (here & (section_ids == 0))
    local_shift = jnp.where(section_ids == 0, offset, -offset)
    copies, partner = exchange(0, local_shift)
    pending = [strip_copies, copies]
    shift = jnp.where(measured, local_shift, -partner)
    for component in range(2):
        for section in range(2):
            for direction in range(5):
                lane = SECTION * section + P_SIZE * direction
                row = shift[component : component + 1]
                moved = pltpu.roll(row, SLOTS - lane, 1) if lane else row
                match_out[component, section, 0, direction] = moved[:, :P_SIZE]

    def scatter(tile):
        return join_thirds(dot(thirds(jnp.where(matching, tile, 0.0)), owner[...]))

    vertices = lax.broadcasted_iota(jnp.int32, (ROWS, NV), 1)
    column = vertices % V
    left = (column > 0).astype(f32)
    right = (column < V - 1).astype(f32)
    above = (vertices >= V).astype(f32)
    below = (vertices < NV - V).astype(f32)
    field_rows = lax.broadcasted_iota(jnp.int32, (ROWS, NV), 0)
    spring = jnp.where(field_rows // 2 % 2 == 0, stiffness[0, 0, 0], stiffness[0, 0, 1])
    used = dot(jnp.where(matching, 1.0, 0.0).astype(bf16), owner[...])
    diagonal = anchor_weight + spring * (left + right + above + below) + used
    inverse = 1.0 / diagonal

    def gather(field):
        return join_thirds(dot(thirds(field), owner_t[...]))

    def around(field):
        return spring * (
            pltpu.roll(field, 1, 1) * left
            + pltpu.roll(field, NV - 1, 1) * right
            + pltpu.roll(field, V, 1) * above
            + pltpu.roll(field, NV - V, 1) * below
        )

    def smooth(number, field):
        copies, partner = exchange(number, gather(field))
        pending.append(copies)
        return (around(field) + scatter(partner)) * inverse

    right_side = scatter(shift)
    base0 = right_side * inverse
    image0 = smooth(1, base0)
    base1 = image0
    image1 = smooth(2, base1)
    base2 = 2.0 * image1 - base0
    bases = (base0, base1, base2)
    applied = (
        diagonal * (base0 - image0),
        diagonal * (base1 - image1),
        diagonal * base2 - around(base2),
    )
    pairs = ((0, 0), (0, 1), (0, 2), (1, 1), (1, 2), (2, 2))
    terms = [applied[one] * bases[other] for one, other in pairs]
    terms += [base * right_side for base in bases]
    partial = jnp.concatenate([jnp.sum(term, axis=0, keepdims=True) for term in terms], axis=0)
    partial = sum(partial[:, start : start + SLOTS] for start in range(0, NV, SLOTS))
    tile = gather(base2)
    values = jnp.where(section_ids[:2] == 0, tile[:2], tile[2:4])
    filler = jnp.zeros((DOTS - len(terms) - 2, SLOTS), f32)
    partial = jnp.concatenate([partial, values, filler], axis=0)
    last = pairs.index((2, 2))

    def couple(entries, low, high, direction, reach):
        product = jnp.where(direction_ids[:1] == direction, low * pltpu.roll(high, reach, 1), 0.0)
        product = 4.0 * jnp.sum(product, axis=0, keepdims=True)
        ids = lax.broadcasted_iota(jnp.int32, entries.shape, 0)
        return entries - jnp.where(ids == last, product, 0.0)

    cross = jnp.where(section_ids[:1] == 0, values, 0.0)
    partial = couple(partial, cross, values, 4, SECTION)

    def all_sum(value, axis, me, count, buffer, send, recv):
        buffer[me] = value
        copies = []
        for offset in range(1, count):
            peer = {"ty": ty, "tx": tx}
            peer[axis] = lax.rem(me + offset, count)
            copy = pltpu.make_async_remote_copy(
                src_ref=buffer.at[me],
                dst_ref=buffer.at[me],
                send_sem=send.at[offset],
                recv_sem=recv.at[offset],
                device_id=peer,
                device_id_type=MESH,
            )
            copy.start()
            copies.append(copy)
        for copy in copies:
            copy.wait_recv()
        total = buffer[0, :DOTS]
        for number in range(1, count):
            total = total + buffer[number, :DOTS]
        return copies, total

    x_copies, partial = all_sum(partial, "tx", tx, ntx, dots_x, x_send, x_recv)
    start = len(terms)
    values = [dots_x[number, start : start + 2] for number in range(ntx)]
    held = jnp.concatenate(values, axis=0)
    if ntx > 1:
        partial = couple(partial, held[:-2], held[2:], 0, SLOTS - P_SIZE)
    missing = dots_y.shape[1] - DOTS - 2 * ntx
    filler = [jnp.zeros((missing, SLOTS), f32)] if missing else []
    tall = jnp.concatenate([partial, held] + filler, axis=0)
    y_copies, partial = all_sum(tall, "ty", ty, nty, dots_y, y_send, y_recv)
    for number in range(nty - 1):
        partial = couple(
            partial, dots_y[number, DOTS:], dots_y[number + 1, DOTS:], 2, SLOTS - P_SIZE
        )
    entries = jnp.sum(partial, axis=1, keepdims=True)
    k00, k01, k02, k11, k12, k22, b0, b1, b2 = (
        entries[number : number + 1] for number in range(len(terms))
    )
    low10, low20 = k01 / k00, k02 / k00
    pivot1 = k11 - low10 * k01
    rest12 = k12 - low10 * k02
    low21 = rest12 / pivot1
    pivot2 = k22 - low20 * k02 - low21 * rest12
    b1 = b1 - low10 * b0
    b2 = b2 - low20 * b0 - low21 * b1
    y2 = b2 / pivot2
    y1 = b1 / pivot1 - low21 * y2
    y0 = b0 / k00 - low10 * y1 - low20 * y2
    result = y0 * base0 + y1 * base1 + y2 * base2
    for component in range(2):
        for section in range(2):
            row = 2 * section + component
            vertex_out[component, section, 0] = result[row : row + 1]

    for copies in pending:
        wait_sent(copies)
    for copy in x_copies + y_copies:
        copy.wait_send()


def local(nty, ntx, strips, centers, match_lists, match_counts, spring_stiffness):
    constants = [jnp.asarray(table) for table in tables()]
    sections = strips.shape[0]
    patches = len(BATCHES) * P_SIZE
    vmem = pl.BlockSpec(memory_space=pltpu.VMEM)
    hbm = pl.BlockSpec(memory_space=pltpu.HBM)
    dma = pltpu.SemaphoreType.DMA
    match_lists = jnp.swapaxes(match_lists, 4, 5)
    spring_stiffness = spring_stiffness.transpose(1, 2, 0)
    operands = (strips, centers, match_lists, match_counts, spring_stiffness, *constants)
    tall = DOTS + -(-2 * ntx // 8) * 8
    vertex_shift, match_shift = pl.pallas_call(
        functools.partial(kernel, nty, ntx),
        out_shape=(
            pltpu.VMEM((2, sections, 1, 1, NV), f32),
            pltpu.VMEM((2, sections, 1, 5, 1, P_SIZE), f32),
        ),
        in_specs=[hbm] * len(operands),
        out_specs=(vmem, vmem),
        scratch_shapes=[
            pltpu.VMEM(match_lists.shape, jnp.int32),
            pltpu.SMEM(match_counts.shape, jnp.int32),
            pltpu.SMEM(spring_stiffness.shape, f32),
            *[pltpu.VMEM(table.shape, bf16) for table in constants],
            pltpu.VMEM((W, 2 * W), f32),
            pltpu.VMEM((NV, SLOTS), bf16),
            pltpu.VMEM((patches, W, W), bf16),
            pltpu.VMEM((patches, W, W), bf16),
            pltpu.VMEM((patches // GROUP, 2 * GROUP, W), f32),
            pltpu.VMEM((SLOTS, NV), bf16),
            pltpu.VMEM((EXCHANGES, ROWS, SLOTS), f32),
            pltpu.VMEM((EXCHANGES, 4, ROWS, SLOTS), f32),
            pltpu.VMEM((ntx, DOTS, SLOTS), f32),
            pltpu.VMEM((nty, tall, SLOTS), f32),
            dma((12,)),
            dma((4,)),
            dma((4,)),
            dma((EXCHANGES, 4)),
            dma((EXCHANGES, 4)),
            dma((ntx,)),
            dma((ntx,)),
            dma((nty,)),
            dma((nty,)),
        ],
        compiler_params=pltpu.CompilerParams(
            collective_id=0, has_side_effects=True, vmem_limit_bytes=62 * 1024 * 1024
        ),
    )(*operands)
    return vertex_shift, jnp.swapaxes(match_shift, 3, 4)


def solution(mesh):
    return jax.shard_map(
        functools.partial(local, mesh.shape["ty"], mesh.shape["tx"]),
        mesh=mesh,
        in_specs=(
            P(None, "ty", "tx", None, None, None, None),
            P(None, "ty", "tx", None, None, None),
            P(None, "ty", "tx", None, None, None),
            P(None, "ty", "tx", None),
            P(None, "ty", "tx"),
        ),
        out_specs=(P(None, None, "ty", "tx", None), P(None, None, "ty", "tx", None, None)),
        check_vma=False,
    )
```

```python
import functools

import jax
import jax.numpy as jnp
import ml_dtypes
import numpy as np
from jax import lax
from jax.experimental import pallas as pl
from jax.experimental.pallas import tpu as pltpu
from jax.sharding import PartitionSpec as P

P_SIZE = 8
W = 128
V = 32
HALF = W // 2
NV = V * V
GROUP = 4
SLOTS = 128
SECTION = SLOTS // 2
ROWS = 8
EXCHANGES = 3
DOTS = 16

anchor_weight = 0.05
epsilon = 1e-06

EDGES = ((0, 0), (1, 1), (0, 2), (1, 3))
PARTS = tuple(range(0, P_SIZE, GROUP))
GROUPS = tuple((0, 4, start) for start in PARTS) + tuple(
    (section, direction, start) for start in PARTS for section, direction in EDGES
)

f32 = jnp.float32
bf16 = jnp.bfloat16
MESH = pl.DeviceIdType.MESH


def split_table(table):
    high = table.astype(ml_dtypes.bfloat16)
    low = (table - high.astype(np.float64)).astype(ml_dtypes.bfloat16)
    return high, low


def tables():
    indices = np.arange(W)
    angles = (indices[:, None] * indices[None, :] % W) * (2.0 * np.pi / W)
    cos, sin = np.cos(angles), np.sin(angles)
    analysis = np.concatenate([cos[:HALF], cos[HALF : HALF + 1], sin[1:HALF]])
    high, low = split_table(analysis)
    first = np.concatenate([high, low], axis=1)
    high, low = split_table(np.block([[cos, sin], [-sin, cos]]))
    middle = np.concatenate([high, high, low], axis=0)
    factors = np.full((W, 1), 2.0)
    factors[0] = factors[HALF] = 1.0
    factors[HALF + 1 :] = -2.0
    high, low = split_table((analysis * factors).T / float(W * W * W))
    last = np.concatenate([high, high, low], axis=1)
    return first, middle, last


def lag_values(shape, dimension):
    ids = lax.broadcasted_iota(jnp.int32, shape, dimension)
    lags = jnp.where(ids < HALF, ids, jnp.where(ids == HALF, 0, ids - W))
    return lags.astype(f32)


def dot(left, right, contract=((1,), (0,))):
    return lax.dot_general(left, right, (contract, ((), ())), preferred_element_type=f32)


def halves(values):
    high = values.astype(bf16)
    low = (values - high.astype(f32)).astype(bf16)
    return high, low


def thirds(values):
    first = values.astype(bf16)
    rest = values - first.astype(f32)
    second = rest.astype(bf16)
    third = (rest - second.astype(f32)).astype(bf16)
    return jnp.concatenate([first, second, third], axis=0)


def join_thirds(values):
    rows = values.shape[0] // 3
    return values[:rows] + (values[rows : 2 * rows] + values[2 * rows :])


def put_first_row(row, block):
    head = block[:8]
    ids = lax.broadcasted_iota(jnp.int32, head.shape, 0)
    return jnp.concatenate([jnp.where(ids == 0, row, head), block[8:]], axis=0)


def analyse(step, own, far, first_ref, middle_ref):
    zero_row = jnp.zeros((1, W), f32)
    blocks, own_nyquist, far_nyquist = [], [], []
    for inner in range(GROUP):
        pixels = jnp.concatenate([own[step * GROUP + inner], far[step * GROUP + inner]], axis=1)
        spread = dot(first_ref[...], jnp.concatenate([pixels, pixels], axis=0))
        for lanes, rows in ((0, own_nyquist), (W, far_nyquist)):
            upper = spread[:HALF, lanes : lanes + W]
            lower = spread[HALF:, lanes : lanes + W]
            rows.append(lower[:1])
            blocks.append(jnp.concatenate([upper, put_first_row(zero_row, lower)], axis=1))
    filler = jnp.zeros((8 - GROUP, W), f32)
    nyquist = jnp.concatenate(own_nyquist + [filler] + far_nyquist + [filler], axis=0)
    blocks.append(jnp.concatenate([nyquist, jnp.zeros_like(nyquist)], axis=1))
    high, low = halves(jnp.concatenate(blocks, axis=0))
    spectra = dot(jnp.concatenate([high, low, high], axis=1), middle_ref[...])

    def cross(one, other):
        real = one[:, :W] * other[:, :W] + one[:, W:] * other[:, W:]
        imag = one[:, :W] * other[:, W:] - one[:, W:] * other[:, :W]
        return jnp.concatenate([real, imag], axis=1)

    products = [
        cross(spectra[start : start + HALF], spectra[start + HALF : start + W])
        for start in range(0, GROUP * W, W)
    ]
    start = GROUP * W
    products.append(cross(spectra[start : start + 8], spectra[start + 8 : start + 16]))
    products.append(jnp.zeros((8, 2 * W), f32))
    return halves(jnp.concatenate(products, axis=0))


def synthesise(step, products, middle_ref, last_ref, lag_ref, sums):
    high, low = products
    waves = dot(jnp.concatenate([high, low, high], axis=1), middle_ref[...])
    columns = []
    for inner in range(GROUP):
        block = waves[inner * HALF : (inner + 1) * HALF]
        row = waves[GROUP * HALF + inner : GROUP * HALF + inner + 1, :W]
        columns.append(
            jnp.concatenate([block[:, :W], put_first_row(row, block[:, W:])], axis=0)
        )
    totals, toward = [], []
    lag = lag_ref[...]
    for inner in range(0, GROUP, 2):
        high, low = halves(jnp.concatenate(columns[inner : inner + 2], axis=1))
        surface = dot(last_ref[...], jnp.concatenate([high, low, high], axis=0))
        squared = surface * surface
        weight = squared * squared
        total = jnp.sum(weight, axis=0, keepdims=True)
        moment = jnp.sum(weight * lag, axis=0, keepdims=True)
        totals += [total[:, :W], total[:, W:]]
        toward += [moment[:, :W], moment[:, W:]]
    sums[step] = jnp.concatenate(totals + toward, axis=0)


def kernel(
    nty,
    ntx,
    strips,
    centers,
    lists_in,
    counts_in,
    stiffness_in,
    first_in,
    middle_in,
    last_in,
    vertex_out,
    match_out,
    lists,
    counts,
    stiffness,
    first_ref,
    middle_ref,
    last_ref,
    lag_rows,
    owner_t,
    own,
    far,
    sums,
    owner,
    sent,
    received,
    dots_x,
    dots_y,
    local_sem,
    strip_send,
    strip_recv,
    value_send,
    value_recv,
    x_send,
    x_recv,
    y_send,
    y_recv,
):
    ty, tx = lax.axis_index("ty"), lax.axis_index("tx")
    targets = (
        {"ty": ty, "tx": tx - 1},
        {"ty": ty, "tx": tx + 1},
        {"ty": ty - 1, "tx": tx},
        {"ty": ty + 1, "tx": tx},
    )
    west, east, north, south = tx > 0, tx < ntx - 1, ty > 0, ty < nty - 1
    sends = (west, east, north, south)
    receives = (east, west, south, north)

    def patches(ref, group):
        return ref.at[pl.ds(GROUPS.index(group) * GROUP, GROUP)]

    def slots(ref, start):
        return ref.at[pl.ds(start, GROUP)]

    local_pairs = []
    for start in PARTS:
        local_pairs += [
            (slots(centers.at[0, 0, 0], start), patches(own, (0, 4, start))),
            (slots(centers.at[1, 0, 0], start), patches(far, (0, 4, start))),
        ]
    local_pairs += [
        (first_in, first_ref),
        (middle_in, middle_ref),
        (last_in, last_ref),
        (lists_in, lists),
        (counts_in, counts),
        (stiffness_in, stiffness),
    ]
    first_edge = len(local_pairs)
    for start in PARTS:
        for section, direction in EDGES:
            kept = own if direction % 2 == 0 else far
            source = slots(strips.at[section, 0, 0, direction], start)
            local_pairs.append((source, patches(kept, (section, direction, start))))
    local_copies = [
        pltpu.make_async_copy(source, target, local_sem.at[number])
        for number, (source, target) in enumerate(local_pairs)
    ]
    landing, strip_copies = [], []
    for part, start in enumerate(PARTS):
        places = [
            patches(far if direction % 2 == 0 else own, (section, direction, start))
            for section, direction in EDGES
        ]
        landing.append(places)
        strip_copies.append(
            [
                pltpu.make_async_remote_copy(
                    src_ref=slots(strips.at[section, 0, 0, direction ^ 1], start),
                    dst_ref=places[number],
                    send_sem=strip_send.at[part, number],
                    recv_sem=strip_recv.at[part, number],
                    device_id=targets[number],
                    device_id_type=MESH,
                )
                for number, (section, direction) in enumerate(EDGES)
            ]
        )
    barrier = pltpu.get_barrier_semaphore()
    for offset in range(1, ntx):
        peer = {"ty": ty, "tx": lax.rem(tx + offset, ntx)}
        pl.semaphore_signal(barrier, inc=1, device_id=peer, device_id_type=MESH)
    for offset in range(1, nty):
        peer = {"ty": lax.rem(ty + offset, nty), "tx": tx}
        pl.semaphore_signal(barrier, inc=1, device_id=peer, device_id_type=MESH)
    for copy in local_copies:
        copy.start()
    pl.semaphore_wait(barrier, ntx + nty - 2)

    def start_all(copies):
        for number in range(4):

            @pl.when(sends[number])
            def _():
                copies[number].start()

    def wait_all(copies, numbers):
        for number in numbers:

            @pl.when(receives[number])
            def _():
                copies[number].wait_recv()

    def wait_sent(copies):
        for number in range(4):

            @pl.when(sends[number])
            def _():
                copies[number].wait_send()

    for copies in strip_copies:
        start_all(copies)
    for number in range(4):

        @pl.when(jnp.logical_not(receives[number]))
        def _():
            for places in landing:
                places[number][...] = jnp.zeros(places[number].shape, bf16)
            for exchanged in range(EXCHANGES):
                received[exchanged, number] = jnp.zeros((ROWS, SLOTS), f32)

    for copy in local_copies[:first_edge]:
        copy.wait()
    lag_rows[...] = lag_values((W, 2 * W), 0)
    lanes = lax.broadcasted_iota(jnp.int32, (ROWS, SLOTS), 1)
    rows = lax.broadcasted_iota(jnp.int32, (ROWS, SLOTS), 0)
    direction_ids = lanes % SECTION // P_SIZE
    section_ids = lanes // SECTION
    matching = section_ids == rows // 2 % 2
    mine, limit = [], jnp.zeros((1, SLOTS), jnp.int32)
    for section in range(2):
        for direction in range(5):
            mine.append(lists[section, 0, 0, direction, 0:1, :])
            inside = (direction_ids[:1] == direction) & (section_ids[:1] == section)
            limit = jnp.where(inside, counts[section, 0, 0, direction], limit)
        mine.append(jnp.zeros((1, SECTION - 5 * P_SIZE), jnp.int32))
    mine = jnp.concatenate(mine, axis=1)
    mine = jnp.where(lanes[:1] % P_SIZE < limit, mine, -1)
    owner_t[...] = jnp.where(
        lax.broadcasted_iota(jnp.int32, (NV, SLOTS), 0) == mine, 1.0, 0.0
    ).astype(bf16)
    square = (SLOTS, SLOTS)
    same = lax.broadcasted_iota(jnp.int32, square, 0) == lax.broadcasted_iota(jnp.int32, square, 1)
    turned = jnp.sum(jnp.where(same, mine.astype(f32), 0.0), axis=1, keepdims=True)
    owner[...] = jnp.where(
        lax.broadcasted_iota(jnp.int32, (SLOTS, NV), 1) == turned.astype(jnp.int32), 1.0, 0.0
    ).astype(bf16)

    vertices = lax.broadcasted_iota(jnp.int32, (ROWS, NV), 1)
    column = vertices % V
    left = (column > 0).astype(f32)
    right = (column < V - 1).astype(f32)
    above = (vertices >= V).astype(f32)
    below = (vertices < NV - V).astype(f32)
    field_rows = lax.broadcasted_iota(jnp.int32, (ROWS, NV), 0)
    spring = jnp.where(field_rows // 2 % 2 == 0, stiffness[0, 0, 0], stiffness[0, 0, 1])
    used = dot(jnp.where(matching, 1.0, 0.0).astype(bf16), owner[...])
    diagonal = anchor_weight + spring * (left + right + above + below) + used
    inverse = 1.0 / diagonal

    def analysis(step):
        return analyse(step, own, far, first_ref, middle_ref)

    def synthesis(step, products):
        synthesise(step, products, middle_ref, last_ref, lag_rows, sums)

    def steps(low, high, products):
        def body(step, held):
            fresh = analysis(step + 1)
            synthesis(step, held)
            return fresh

        return lax.fori_loop(low, high, body, products)

    done = len(PARTS)
    products = steps(0, done - 1, analysis(0))
    for copy in local_copies[first_edge:]:
        copy.wait()
    for copies in strip_copies:
        wait_all(copies, range(4))
        products = steps(done - 1, done + len(EDGES) - 1, products)
        done += len(EDGES)
    synthesis(done - 1, products)

    def exchange(number, tile, meanwhile=lambda: None):
        sent[number] = tile
        copies = [
            pltpu.make_async_remote_copy(
                src_ref=sent.at[number],
                dst_ref=received.at[number, way],
                send_sem=value_send.at[number, way],
                recv_sem=value_recv.at[number, way],
                device_id=targets[way],
                device_id_type=MESH,
            )
            for way in range(4)
        ]
        start_all(copies)
        partner = pltpu.roll(pltpu.roll(tile, SECTION, 1), 2, 0)
        beside = meanwhile()
        wait_all(copies, range(4))
        for direction in range(4):
            shift = SLOTS - P_SIZE if direction % 2 == 0 else P_SIZE
            moved = pltpu.roll(received[number, direction], shift, 1)
            partner = jnp.where(direction_ids == direction, moved, partner)
        pending.append(copies)
        return partner, beside

    shape = (sums.shape[0] * sums.shape[1], SLOTS)
    stacked = sums[...].reshape(shape)
    row_ids = lax.broadcasted_iota(jnp.int32, shape, 0)
    step_ids, inner_ids = row_ids // (2 * GROUP), row_ids % (2 * GROUP)
    first_lane = jnp.zeros(shape, jnp.int32)
    for number, (section, direction, start) in enumerate(GROUPS):
        lane = SECTION * section + P_SIZE * direction + start
        first_lane = jnp.where(step_ids == number, lane, first_lane)
    place = first_lane + inner_ids % GROUP
    placed = place == lax.broadcasted_iota(jnp.int32, shape, 1)
    is_total = placed & (inner_ids < GROUP)
    is_moment = placed & (inner_ids >= GROUP)
    plain = jnp.sum(stacked, axis=1, keepdims=True)
    lagged = jnp.sum(stacked * lag_values((1, W), 1), axis=1, keepdims=True)
    total = jnp.sum(jnp.where(is_total, plain, 0.0), axis=0, keepdims=True) + epsilon
    toward_cols = jnp.sum(jnp.where(is_total, lagged, 0.0), axis=0, keepdims=True)
    toward_rows = jnp.sum(jnp.where(is_moment, plain, 0.0), axis=0, keepdims=True)
    offset = jnp.where(rows % 2 == 0, toward_rows / total, toward_cols / total) * (2.0 / W)
    here = (direction_ids == 4) | (direction_ids % 2 == section_ids)
    measured = (here & (direction_ids < 4)) | (here & (section_ids == 0))
    local_shift = jnp.where(section_ids == 0, offset, -offset)
    pending = list(strip_copies)
    partner, _ = exchange(0, local_shift)
    shift = jnp.where(measured, local_shift, -partner)
    def write_shift():
        for component in range(2):
            for section in range(2):
                for direction in range(5):
                    lane = SECTION * section + P_SIZE * direction
                    row = shift[component : component + 1]
                    moved = pltpu.roll(row, SLOTS - lane, 1) if lane else row
                    match_out[component, section, 0, direction] = moved[:, :P_SIZE]

    def scatter(tile):
        return join_thirds(dot(thirds(jnp.where(matching, tile, 0.0)), owner[...]))

    def gather(field):
        return join_thirds(dot(thirds(field), owner_t[...]))

    def around(field):
        return spring * (
            pltpu.roll(field, 1, 1) * left
            + pltpu.roll(field, NV - 1, 1) * right
            + pltpu.roll(field, V, 1) * above
            + pltpu.roll(field, NV - V, 1) * below
        )

    def smooth(number, field, also=lambda: None):
        def meanwhile():
            also()
            return around(field)

        partner, near = exchange(number, gather(field), meanwhile)
        return (near + scatter(partner)) * inverse

    right_side = scatter(shift)
    base0 = right_side * inverse
    image0 = smooth(1, base0, write_shift)
    base1 = image0
    image1 = smooth(2, base1)
    base2 = 2.0 * image1 - base0
    bases = (base0, base1, base2)
    applied = (
        diagonal * (base0 - image0),
        diagonal * (base1 - image1),
        diagonal * base2 - around(base2),
    )
    pairs = ((0, 0), (0, 1), (0, 2), (1, 1), (1, 2), (2, 2))
    terms = [applied[one] * bases[other] for one, other in pairs]
    terms += [base * right_side for base in bases]
    partial = jnp.concatenate([jnp.sum(term, axis=0, keepdims=True) for term in terms], axis=0)
    partial = sum(partial[:, start : start + SLOTS] for start in range(0, NV, SLOTS))
    tile = gather(base2)
    values = jnp.where(section_ids[:2] == 0, tile[:2], tile[2:4])
    filler = jnp.zeros((DOTS - len(terms) - 2, SLOTS), f32)
    partial = jnp.concatenate([partial, values, filler], axis=0)
    last = pairs.index((2, 2))

    def couple(entries, low, high, direction, reach):
        product = jnp.where(direction_ids[:1] == direction, low * pltpu.roll(high, reach, 1), 0.0)
        product = 4.0 * jnp.sum(product, axis=0, keepdims=True)
        ids = lax.broadcasted_iota(jnp.int32, entries.shape, 0)
        return entries - jnp.where(ids == last, product, 0.0)

    cross = jnp.where(section_ids[:1] == 0, values, 0.0)
    partial = couple(partial, cross, values, 4, SECTION)

    def all_sum(value, axis, me, count, buffer, send, recv):
        buffer[me] = value
        copies = []
        for offset in range(1, count):
            peer = {"ty": ty, "tx": tx}
            peer[axis] = lax.rem(me + offset, count)
            copy = pltpu.make_async_remote_copy(
                src_ref=buffer.at[me],
                dst_ref=buffer.at[me],
                send_sem=send.at[offset],
                recv_sem=recv.at[offset],
                device_id=peer,
                device_id_type=MESH,
            )
            copy.start()
            copies.append(copy)
        for copy in copies:
            copy.wait_recv()
        total = buffer[0, :DOTS]
        for number in range(1, count):
            total = total + buffer[number, :DOTS]
        return copies, total

    x_copies, partial = all_sum(partial, "tx", tx, ntx, dots_x, x_send, x_recv)
    start = len(terms)
    values = [dots_x[number, start : start + 2] for number in range(ntx)]
    held = jnp.concatenate(values, axis=0)
    if ntx > 1:
        partial = couple(partial, held[:-2], held[2:], 0, SLOTS - P_SIZE)
    missing = dots_y.shape[1] - DOTS - 2 * ntx
    filler = [jnp.zeros((missing, SLOTS), f32)] if missing else []
    tall = jnp.concatenate([partial, held] + filler, axis=0)
    y_copies, partial = all_sum(tall, "ty", ty, nty, dots_y, y_send, y_recv)
    for number in range(nty - 1):
        partial = couple(
            partial, dots_y[number, DOTS:], dots_y[number + 1, DOTS:], 2, SLOTS - P_SIZE
        )
    entries = jnp.sum(partial, axis=1, keepdims=True)
    k00, k01, k02, k11, k12, k22, b0, b1, b2 = (
        entries[number : number + 1] for number in range(len(terms))
    )
    low10, low20 = k01 / k00, k02 / k00
    pivot1 = k11 - low10 * k01
    rest12 = k12 - low10 * k02
    low21 = rest12 / pivot1
    pivot2 = k22 - low20 * k02 - low21 * rest12
    b1 = b1 - low10 * b0
    b2 = b2 - low20 * b0 - low21 * b1
    y2 = b2 / pivot2
    y1 = b1 / pivot1 - low21 * y2
    y0 = b0 / k00 - low10 * y1 - low20 * y2
    result = y0 * base0 + y1 * base1 + y2 * base2
    for component in range(2):
        for section in range(2):
            row = 2 * section + component
            vertex_out[component, section, 0] = result[row : row + 1]

    for copies in pending:
        wait_sent(copies)
    for copy in x_copies + y_copies:
        copy.wait_send()


def local(nty, ntx, strips, centers, match_lists, match_counts, spring_stiffness):
    constants = [jnp.asarray(table) for table in tables()]
    sections = strips.shape[0]
    patches = len(GROUPS) * GROUP
    vmem = pl.BlockSpec(memory_space=pltpu.VMEM)
    hbm = pl.BlockSpec(memory_space=pltpu.HBM)
    dma = pltpu.SemaphoreType.DMA
    match_lists = jnp.swapaxes(match_lists, 4, 5)
    spring_stiffness = spring_stiffness.transpose(1, 2, 0)
    operands = (strips, centers, match_lists, match_counts, spring_stiffness, *constants)
    tall = DOTS + -(-2 * ntx // 8) * 8
    vertex_shift, match_shift = pl.pallas_call(
        functools.partial(kernel, nty, ntx),
        out_shape=(
            pltpu.VMEM((2, sections, 1, 1, NV), f32),
            pltpu.VMEM((2, sections, 1, 5, 1, P_SIZE), f32),
        ),
        in_specs=[hbm] * len(operands),
        out_specs=(vmem, vmem),
        scratch_shapes=[
            pltpu.VMEM(match_lists.shape, jnp.int32),
            pltpu.SMEM(match_counts.shape, jnp.int32),
            pltpu.SMEM(spring_stiffness.shape, f32),
            *[pltpu.VMEM(table.shape, bf16) for table in constants],
            pltpu.VMEM((W, 2 * W), f32),
            pltpu.VMEM((NV, SLOTS), bf16),
            pltpu.VMEM((patches, W, W), bf16),
            pltpu.VMEM((patches, W, W), bf16),
            pltpu.VMEM((patches // GROUP, 2 * GROUP, W), f32),
            pltpu.VMEM((SLOTS, NV), bf16),
            pltpu.VMEM((EXCHANGES, ROWS, SLOTS), f32),
            pltpu.VMEM((EXCHANGES, 4, ROWS, SLOTS), f32),
            pltpu.VMEM((ntx, DOTS, SLOTS), f32),
            pltpu.VMEM((nty, tall, SLOTS), f32),
            dma((2 * len(PARTS) + 6 + len(PARTS) * len(EDGES),)),
            dma((len(PARTS), 4)),
            dma((len(PARTS), 4)),
            dma((EXCHANGES, 4)),
            dma((EXCHANGES, 4)),
            dma((ntx,)),
            dma((ntx,)),
            dma((nty,)),
            dma((nty,)),
        ],
        compiler_params=pltpu.CompilerParams(
            collective_id=0, has_side_effects=True, vmem_limit_bytes=62 * 1024 * 1024
        ),
    )(*operands)
    return vertex_shift, jnp.swapaxes(match_shift, 3, 4)


def solution(mesh):
    return jax.shard_map(
        functools.partial(local, mesh.shape["ty"], mesh.shape["tx"]),
        mesh=mesh,
        in_specs=(
            P(None, "ty", "tx", None, None, None, None),
            P(None, "ty", "tx", None, None, None),
            P(None, "ty", "tx", None, None, None),
            P(None, "ty", "tx", None),
            P(None, "ty", "tx"),
        ),
        out_specs=(P(None, None, "ty", "tx", None), P(None, None, "ty", "tx", None, None)),
        check_vma=False,
    )
```

```python
import functools

import jax
import jax.numpy as jnp
import ml_dtypes
import numpy as np
from jax import lax
from jax.experimental import pallas as pl
from jax.experimental.pallas import tpu as pltpu
from jax.sharding import PartitionSpec as P

P_SIZE = 8
W = 128
V = 32
HALF = W // 2
NV = V * V
GROUP = 4
SLOTS = 128
SECTION = SLOTS // 2
ROWS = 8
EXCHANGES = 3
DOTS = 16

anchor_weight = 0.05
epsilon = 1e-06

EDGES = ((0, 0), (1, 1), (0, 2), (1, 3))
PARTS = tuple(range(0, P_SIZE, GROUP))
GROUPS = tuple((0, 4, start) for start in PARTS) + tuple(
    (section, direction, start) for start in PARTS for section, direction in EDGES
)

f32 = jnp.float32
bf16 = jnp.bfloat16
MESH = pl.DeviceIdType.MESH


def split_table(table):
    high = table.astype(ml_dtypes.bfloat16)
    low = (table - high.astype(np.float64)).astype(ml_dtypes.bfloat16)
    return high, low


def tables():
    indices = np.arange(W)
    angles = (indices[:, None] * indices[None, :] % W) * (2.0 * np.pi / W)
    cos, sin = np.cos(angles), np.sin(angles)
    analysis = np.concatenate([cos[:HALF], cos[HALF : HALF + 1], sin[1:HALF]])
    high, low = split_table(analysis)
    first = np.concatenate([high, low], axis=1)
    high, low = split_table(np.block([[cos, sin], [-sin, cos]]))
    middle = np.concatenate([high, high, low], axis=0)
    factors = np.full((W, 1), 2.0)
    factors[0] = factors[HALF] = 1.0
    factors[HALF + 1 :] = -2.0
    high, low = split_table((analysis * factors).T / float(W * W * W))
    last = np.concatenate([high, high, low], axis=1)
    return first, middle, last


def lag_values(shape, dimension):
    ids = lax.broadcasted_iota(jnp.int32, shape, dimension)
    lags = jnp.where(ids < HALF, ids, jnp.where(ids == HALF, 0, ids - W))
    return lags.astype(f32)


def dot(left, right, contract=((1,), (0,))):
    return lax.dot_general(left, right, (contract, ((), ())), preferred_element_type=f32)


def halves(values):
    high = values.astype(bf16)
    low = (values - high.astype(f32)).astype(bf16)
    return high, low


def thirds(values):
    first = values.astype(bf16)
    rest = values - first.astype(f32)
    second = rest.astype(bf16)
    third = (rest - second.astype(f32)).astype(bf16)
    return jnp.concatenate([first, second, third], axis=0)


def join_thirds(values):
    rows = values.shape[0] // 3
    return values[:rows] + (values[rows : 2 * rows] + values[2 * rows :])


def put_first_row(row, block):
    head = block[:8]
    ids = lax.broadcasted_iota(jnp.int32, head.shape, 0)
    return jnp.concatenate([jnp.where(ids == 0, row, head), block[8:]], axis=0)


def analyse(step, own, far, first_ref, middle_ref):
    zero_row = jnp.zeros((1, W), f32)
    blocks, own_nyquist, far_nyquist = [], [], []
    for inner in range(GROUP):
        pixels = jnp.concatenate([own[step * GROUP + inner], far[step * GROUP + inner]], axis=1)
        spread = dot(first_ref[...], jnp.concatenate([pixels, pixels], axis=0))
        for lanes, rows in ((0, own_nyquist), (W, far_nyquist)):
            upper = spread[:HALF, lanes : lanes + W]
            lower = spread[HALF:, lanes : lanes + W]
            rows.append(lower[:1])
            blocks.append(jnp.concatenate([upper, put_first_row(zero_row, lower)], axis=1))
    filler = jnp.zeros((8 - GROUP, W), f32)
    nyquist = jnp.concatenate(own_nyquist + [filler] + far_nyquist + [filler], axis=0)
    blocks.append(jnp.concatenate([nyquist, jnp.zeros_like(nyquist)], axis=1))
    high, low = halves(jnp.concatenate(blocks, axis=0))
    spectra = dot(jnp.concatenate([high, low, high], axis=1), middle_ref[...])

    def cross(one, other):
        real = one[:, :W] * other[:, :W] + one[:, W:] * other[:, W:]
        imag = one[:, :W] * other[:, W:] - one[:, W:] * other[:, :W]
        return jnp.concatenate([real, imag], axis=1)

    products = [
        cross(spectra[start : start + HALF], spectra[start + HALF : start + W])
        for start in range(0, GROUP * W, W)
    ]
    start = GROUP * W
    products.append(cross(spectra[start : start + 8], spectra[start + 8 : start + 16]))
    products.append(jnp.zeros((8, 2 * W), f32))
    return halves(jnp.concatenate(products, axis=0))


def synthesise(step, products, middle_ref, last_ref, lag_ref, sums):
    high, low = products
    waves = dot(jnp.concatenate([high, low, high], axis=1), middle_ref[...])
    columns = []
    for inner in range(GROUP):
        block = waves[inner * HALF : (inner + 1) * HALF]
        row = waves[GROUP * HALF + inner : GROUP * HALF + inner + 1, :W]
        columns.append(
            jnp.concatenate([block[:, :W], put_first_row(row, block[:, W:])], axis=0)
        )
    totals, toward = [], []
    lag = lag_ref[...]
    for inner in range(0, GROUP, 2):
        high, low = halves(jnp.concatenate(columns[inner : inner + 2], axis=1))
        surface = dot(last_ref[...], jnp.concatenate([high, low, high], axis=0))
        squared = surface * surface
        weight = squared * squared
        total = jnp.sum(weight, axis=0, keepdims=True)
        moment = jnp.sum(weight * lag, axis=0, keepdims=True)
        totals += [total[:, :W], total[:, W:]]
        toward += [moment[:, :W], moment[:, W:]]
    sums[step] = jnp.concatenate(totals + toward, axis=0)


def kernel(
    nty,
    ntx,
    strips,
    centers,
    lists_in,
    counts_in,
    stiffness_in,
    first_in,
    middle_in,
    last_in,
    vertex_out,
    match_out,
    lists,
    counts,
    stiffness,
    first_ref,
    middle_ref,
    last_ref,
    lag_rows,
    owner_t,
    own,
    far,
    sums,
    owner,
    sent,
    received,
    dots_x,
    dots_y,
    local_sem,
    strip_send,
    strip_recv,
    value_send,
    value_recv,
    x_send,
    x_recv,
    y_send,
    y_recv,
):
    ty, tx = lax.axis_index("ty"), lax.axis_index("tx")
    targets = (
        {"ty": ty, "tx": tx - 1},
        {"ty": ty, "tx": tx + 1},
        {"ty": ty - 1, "tx": tx},
        {"ty": ty + 1, "tx": tx},
    )
    west, east, north, south = tx > 0, tx < ntx - 1, ty > 0, ty < nty - 1
    sends = (west, east, north, south)
    receives = (east, west, south, north)

    def patches(ref, group):
        return ref.at[pl.ds(GROUPS.index(group) * GROUP, GROUP)]

    def slots(ref, start):
        return ref.at[pl.ds(start, GROUP)]

    local_pairs = []
    for start in PARTS:
        local_pairs += [
            (slots(centers.at[0, 0, 0], start), patches(own, (0, 4, start))),
            (slots(centers.at[1, 0, 0], start), patches(far, (0, 4, start))),
        ]
    local_pairs += [
        (first_in, first_ref),
        (middle_in, middle_ref),
        (last_in, last_ref),
        (lists_in, lists),
        (counts_in, counts),
        (stiffness_in, stiffness),
    ]
    first_edge = len(local_pairs)
    for start in PARTS:
        for section, direction in EDGES:
            kept = own if direction % 2 == 0 else far
            source = slots(strips.at[section, 0, 0, direction], start)
            local_pairs.append((source, patches(kept, (section, direction, start))))
    local_copies = [
        pltpu.make_async_copy(source, target, local_sem.at[number])
        for number, (source, target) in enumerate(local_pairs)
    ]
    landing, strip_copies = [], []
    for part, start in enumerate(PARTS):
        places = [
            patches(far if direction % 2 == 0 else own, (section, direction, start))
            for section, direction in EDGES
        ]
        landing.append(places)
        strip_copies.append(
            [
                pltpu.make_async_remote_copy(
                    src_ref=slots(strips.at[section, 0, 0, direction ^ 1], start),
                    dst_ref=places[number],
                    send_sem=strip_send.at[part, number],
                    recv_sem=strip_recv.at[part, number],
                    device_id=targets[number],
                    device_id_type=MESH,
                )
                for number, (section, direction) in enumerate(EDGES)
            ]
        )
    barrier = pltpu.get_barrier_semaphore()
    for offset in range(1, ntx):
        peer = {"ty": ty, "tx": lax.rem(tx + offset, ntx)}
        pl.semaphore_signal(barrier, inc=1, device_id=peer, device_id_type=MESH)
    for offset in range(1, nty):
        peer = {"ty": lax.rem(ty + offset, nty), "tx": tx}
        pl.semaphore_signal(barrier, inc=1, device_id=peer, device_id_type=MESH)
    for copy in local_copies:
        copy.start()
    pl.semaphore_wait(barrier, ntx + nty - 2)

    def start_all(copies):
        for number in range(4):

            @pl.when(sends[number])
            def _():
                copies[number].start()

    def wait_all(copies, numbers):
        for number in numbers:

            @pl.when(receives[number])
            def _():
                copies[number].wait_recv()

    def wait_sent(copies):
        for number in range(4):

            @pl.when(sends[number])
            def _():
                copies[number].wait_send()

    for copies in strip_copies:
        start_all(copies)
    for number in range(4):

        @pl.when(jnp.logical_not(receives[number]))
        def _():
            for places in landing:
                places[number][...] = jnp.zeros(places[number].shape, bf16)
            for exchanged in range(EXCHANGES):
                received[exchanged, number] = jnp.zeros((ROWS, SLOTS), f32)

    for copy in local_copies[:first_edge]:
        copy.wait()
    lag_rows[...] = lag_values((W, 2 * W), 0)
    lanes = lax.broadcasted_iota(jnp.int32, (ROWS, SLOTS), 1)
    rows = lax.broadcasted_iota(jnp.int32, (ROWS, SLOTS), 0)
    direction_ids = lanes % SECTION // P_SIZE
    section_ids = lanes // SECTION
    matching = section_ids == rows // 2 % 2
    mine, limit = [], jnp.zeros((1, SLOTS), jnp.int32)
    for section in range(2):
        for direction in range(5):
            mine.append(lists[section, 0, 0, direction, 0:1, :])
            inside = (direction_ids[:1] == direction) & (section_ids[:1] == section)
            limit = jnp.where(inside, counts[section, 0, 0, direction], limit)
        mine.append(jnp.zeros((1, SECTION - 5 * P_SIZE), jnp.int32))
    mine = jnp.concatenate(mine, axis=1)
    mine = jnp.where(lanes[:1] % P_SIZE < limit, mine, -1)
    owner_t[...] = jnp.where(
        lax.broadcasted_iota(jnp.int32, (NV, SLOTS), 0) == mine, 1.0, 0.0
    ).astype(bf16)
    square = (SLOTS, SLOTS)
    same = lax.broadcasted_iota(jnp.int32, square, 0) == lax.broadcasted_iota(jnp.int32, square, 1)
    turned = jnp.sum(jnp.where(same, mine.astype(f32), 0.0), axis=1, keepdims=True)
    owner[...] = jnp.where(
        lax.broadcasted_iota(jnp.int32, (SLOTS, NV), 1) == turned.astype(jnp.int32), 1.0, 0.0
    ).astype(bf16)

    vertices = lax.broadcasted_iota(jnp.int32, (ROWS, NV), 1)
    column = vertices % V
    left = (column > 0).astype(f32)
    right = (column < V - 1).astype(f32)
    above = (vertices >= V).astype(f32)
    below = (vertices < NV - V).astype(f32)
    field_rows = lax.broadcasted_iota(jnp.int32, (ROWS, NV), 0)
    spring = jnp.where(field_rows // 2 % 2 == 0, stiffness[0, 0, 0], stiffness[0, 0, 1])
    used = dot(jnp.where(matching, 1.0, 0.0).astype(bf16), owner[...])
    diagonal = anchor_weight + spring * (left + right + above + below) + used
    inverse = 1.0 / diagonal

    def analysis(step):
        return analyse(step, own, far, first_ref, middle_ref)

    def synthesis(step, products):
        synthesise(step, products, middle_ref, last_ref, lag_rows, sums)

    def steps(low, high, products):
        def body(step, held):
            fresh = analysis(step + 1)
            synthesis(step, held)
            return fresh

        unroll = 2 if (high - low) % 2 == 0 else 1
        return lax.fori_loop(low, high, body, products, unroll=unroll)

    done = len(PARTS)
    products = steps(0, done - 1, analysis(0))
    for copy in local_copies[first_edge:]:
        copy.wait()
    for copies in strip_copies:
        wait_all(copies, range(4))
        products = steps(done - 1, done + len(EDGES) - 1, products)
        done += len(EDGES)
    synthesis(done - 1, products)

    def exchange(number, tile, meanwhile=lambda: None):
        sent[number] = tile
        copies = [
            pltpu.make_async_remote_copy(
                src_ref=sent.at[number],
                dst_ref=received.at[number, way],
                send_sem=value_send.at[number, way],
                recv_sem=value_recv.at[number, way],
                device_id=targets[way],
                device_id_type=MESH,
            )
            for way in range(4)
        ]
        start_all(copies)
        partner = pltpu.roll(pltpu.roll(tile, SECTION, 1), 2, 0)
        beside = meanwhile()
        wait_all(copies, range(4))
        for direction in range(4):
            shift = SLOTS - P_SIZE if direction % 2 == 0 else P_SIZE
            moved = pltpu.roll(received[number, direction], shift, 1)
            partner = jnp.where(direction_ids == direction, moved, partner)
        pending.append(copies)
        return partner, beside

    shape = (sums.shape[0] * sums.shape[1], SLOTS)
    stacked = sums[...].reshape(shape)
    row_ids = lax.broadcasted_iota(jnp.int32, shape, 0)
    step_ids, inner_ids = row_ids // (2 * GROUP), row_ids % (2 * GROUP)
    first_lane = jnp.zeros(shape, jnp.int32)
    for number, (section, direction, start) in enumerate(GROUPS):
        lane = SECTION * section + P_SIZE * direction + start
        first_lane = jnp.where(step_ids == number, lane, first_lane)
    place = first_lane + inner_ids % GROUP
    placed = place == lax.broadcasted_iota(jnp.int32, shape, 1)
    is_total = placed & (inner_ids < GROUP)
    is_moment = placed & (inner_ids >= GROUP)
    plain = jnp.sum(stacked, axis=1, keepdims=True)
    lagged = jnp.sum(stacked * lag_values((1, W), 1), axis=1, keepdims=True)
    total = jnp.sum(jnp.where(is_total, plain, 0.0), axis=0, keepdims=True) + epsilon
    toward_cols = jnp.sum(jnp.where(is_total, lagged, 0.0), axis=0, keepdims=True)
    toward_rows = jnp.sum(jnp.where(is_moment, plain, 0.0), axis=0, keepdims=True)
    offset = jnp.where(rows % 2 == 0, toward_rows / total, toward_cols / total) * (2.0 / W)
    here = (direction_ids == 4) | (direction_ids % 2 == section_ids)
    measured = (here & (direction_ids < 4)) | (here & (section_ids == 0))
    local_shift = jnp.where(section_ids == 0, offset, -offset)
    pending = list(strip_copies)
    partner, _ = exchange(0, local_shift)
    shift = jnp.where(measured, local_shift, -partner)
    def write_shift():
        for component in range(2):
            for section in range(2):
                for direction in range(5):
                    lane = SECTION * section + P_SIZE * direction
                    row = shift[component : component + 1]
                    moved = pltpu.roll(row, SLOTS - lane, 1) if lane else row
                    match_out[component, section, 0, direction] = moved[:, :P_SIZE]

    def scatter(tile):
        return join_thirds(dot(thirds(jnp.where(matching, tile, 0.0)), owner[...]))

    def gather(field):
        return join_thirds(dot(thirds(field), owner_t[...]))

    def around(field):
        return spring * (
            pltpu.roll(field, 1, 1) * left
            + pltpu.roll(field, NV - 1, 1) * right
            + pltpu.roll(field, V, 1) * above
            + pltpu.roll(field, NV - V, 1) * below
        )

    def smooth(number, field, also=lambda: None):
        def meanwhile():
            also()
            return around(field)

        partner, near = exchange(number, gather(field), meanwhile)
        return (near + scatter(partner)) * inverse

    right_side = scatter(shift)
    base0 = right_side * inverse
    image0 = smooth(1, base0, write_shift)
    base1 = image0
    image1 = smooth(2, base1)
    base2 = 2.0 * image1 - base0
    bases = (base0, base1, base2)
    applied = (
        diagonal * (base0 - image0),
        diagonal * (base1 - image1),
        diagonal * base2 - around(base2),
    )
    pairs = ((0, 0), (0, 1), (0, 2), (1, 1), (1, 2), (2, 2))
    terms = [applied[one] * bases[other] for one, other in pairs]
    terms += [base * right_side for base in bases]
    partial = jnp.concatenate([jnp.sum(term, axis=0, keepdims=True) for term in terms], axis=0)
    partial = sum(partial[:, start : start + SLOTS] for start in range(0, NV, SLOTS))
    tile = gather(base2)
    values = jnp.where(section_ids[:2] == 0, tile[:2], tile[2:4])
    filler = jnp.zeros((DOTS - len(terms) - 2, SLOTS), f32)
    partial = jnp.concatenate([partial, values, filler], axis=0)
    last = pairs.index((2, 2))

    def couple(entries, low, high, direction, reach):
        product = jnp.where(direction_ids[:1] == direction, low * pltpu.roll(high, reach, 1), 0.0)
        product = 4.0 * jnp.sum(product, axis=0, keepdims=True)
        ids = lax.broadcasted_iota(jnp.int32, entries.shape, 0)
        return entries - jnp.where(ids == last, product, 0.0)

    cross = jnp.where(section_ids[:1] == 0, values, 0.0)
    partial = couple(partial, cross, values, 4, SECTION)

    def all_sum(value, axis, me, count, buffer, send, recv):
        buffer[me] = value
        copies = []
        for offset in range(1, count):
            peer = {"ty": ty, "tx": tx}
            peer[axis] = lax.rem(me + offset, count)
            copy = pltpu.make_async_remote_copy(
                src_ref=buffer.at[me],
                dst_ref=buffer.at[me],
                send_sem=send.at[offset],
                recv_sem=recv.at[offset],
                device_id=peer,
                device_id_type=MESH,
            )
            copy.start()
            copies.append(copy)
        for copy in copies:
            copy.wait_recv()
        total = buffer[0, :DOTS]
        for number in range(1, count):
            total = total + buffer[number, :DOTS]
        return copies, total

    x_copies, partial = all_sum(partial, "tx", tx, ntx, dots_x, x_send, x_recv)
    start = len(terms)
    values = [dots_x[number, start : start + 2] for number in range(ntx)]
    held = jnp.concatenate(values, axis=0)
    if ntx > 1:
        partial = couple(partial, held[:-2], held[2:], 0, SLOTS - P_SIZE)
    missing = dots_y.shape[1] - DOTS - 2 * ntx
    filler = [jnp.zeros((missing, SLOTS), f32)] if missing else []
    tall = jnp.concatenate([partial, held] + filler, axis=0)
    y_copies, partial = all_sum(tall, "ty", ty, nty, dots_y, y_send, y_recv)
    for number in range(nty - 1):
        partial = couple(
            partial, dots_y[number, DOTS:], dots_y[number + 1, DOTS:], 2, SLOTS - P_SIZE
        )
    entries = jnp.sum(partial, axis=1, keepdims=True)
    k00, k01, k02, k11, k12, k22, b0, b1, b2 = (
        entries[number : number + 1] for number in range(len(terms))
    )
    low10, low20 = k01 / k00, k02 / k00
    pivot1 = k11 - low10 * k01
    rest12 = k12 - low10 * k02
    low21 = rest12 / pivot1
    pivot2 = k22 - low20 * k02 - low21 * rest12
    b1 = b1 - low10 * b0
    b2 = b2 - low20 * b0 - low21 * b1
    y2 = b2 / pivot2
    y1 = b1 / pivot1 - low21 * y2
    y0 = b0 / k00 - low10 * y1 - low20 * y2
    result = y0 * base0 + y1 * base1 + y2 * base2
    for component in range(2):
        for section in range(2):
            row = 2 * section + component
            vertex_out[component, section, 0] = result[row : row + 1]

    for copies in pending:
        wait_sent(copies)
    for copy in x_copies + y_copies:
        copy.wait_send()


def local(nty, ntx, strips, centers, match_lists, match_counts, spring_stiffness):
    constants = [jnp.asarray(table) for table in tables()]
    sections = strips.shape[0]
    patches = len(GROUPS) * GROUP
    vmem = pl.BlockSpec(memory_space=pltpu.VMEM)
    hbm = pl.BlockSpec(memory_space=pltpu.HBM)
    dma = pltpu.SemaphoreType.DMA
    match_lists = jnp.swapaxes(match_lists, 4, 5)
    spring_stiffness = spring_stiffness.transpose(1, 2, 0)
    operands = (strips, centers, match_lists, match_counts, spring_stiffness, *constants)
    tall = DOTS + -(-2 * ntx // 8) * 8
    vertex_shift, match_shift = pl.pallas_call(
        functools.partial(kernel, nty, ntx),
        out_shape=(
            pltpu.VMEM((2, sections, 1, 1, NV), f32),
            pltpu.VMEM((2, sections, 1, 5, 1, P_SIZE), f32),
        ),
        in_specs=[hbm] * len(operands),
        out_specs=(vmem, vmem),
        scratch_shapes=[
            pltpu.VMEM(match_lists.shape, jnp.int32),
            pltpu.SMEM(match_counts.shape, jnp.int32),
            pltpu.SMEM(spring_stiffness.shape, f32),
            *[pltpu.VMEM(table.shape, bf16) for table in constants],
            pltpu.VMEM((W, 2 * W), f32),
            pltpu.VMEM((NV, SLOTS), bf16),
            pltpu.VMEM((patches, W, W), bf16),
            pltpu.VMEM((patches, W, W), bf16),
            pltpu.VMEM((patches // GROUP, 2 * GROUP, W), f32),
            pltpu.VMEM((SLOTS, NV), bf16),
            pltpu.VMEM((EXCHANGES, ROWS, SLOTS), f32),
            pltpu.VMEM((EXCHANGES, 4, ROWS, SLOTS), f32),
            pltpu.VMEM((ntx, DOTS, SLOTS), f32),
            pltpu.VMEM((nty, tall, SLOTS), f32),
            dma((2 * len(PARTS) + 6 + len(PARTS) * len(EDGES),)),
            dma((len(PARTS), 4)),
            dma((len(PARTS), 4)),
            dma((EXCHANGES, 4)),
            dma((EXCHANGES, 4)),
            dma((ntx,)),
            dma((ntx,)),
            dma((nty,)),
            dma((nty,)),
        ],
        compiler_params=pltpu.CompilerParams(
            collective_id=0, has_side_effects=True, vmem_limit_bytes=62 * 1024 * 1024
        ),
    )(*operands)
    return vertex_shift, jnp.swapaxes(match_shift, 3, 4)


def solution(mesh):
    return jax.shard_map(
        functools.partial(local, mesh.shape["ty"], mesh.shape["tx"]),
        mesh=mesh,
        in_specs=(
            P(None, "ty", "tx", None, None, None, None),
            P(None, "ty", "tx", None, None, None),
            P(None, "ty", "tx", None, None, None),
            P(None, "ty", "tx", None),
            P(None, "ty", "tx"),
        ),
        out_specs=(P(None, None, "ty", "tx", None), P(None, None, "ty", "tx", None, None)),
        check_vma=False,
    )
```
